768 devices in a mesh: grid: 96 (over y, z), mem: 8 (over x, core).
Axes of the slice: x: 4, y: 8, z: 12, core: 2. Of those that a mesh axis runs over, the one named last changes fastest.
Arguments:
- background_elapsed_years: float32 [128, 4, 96, 1440], P('mem', None, 'grid'), may hold values from -6 to 6
- currents: float32 [2, 4, 96, 1440], P(None, None, 'grid'), may hold values from -0.1 to 0.1
- diffusivity: float32 [4, 96, 1440], P(None, 'grid'), may hold values from 0.01 to 0.1
- sea_mask: int32 [96, 1440], P('grid'), may hold values 0 or 1
- observed_cell: int32 [49152], P('grid'), may hold values from 0 to 1439
- measured_layer_number: int32 [49152], P('grid'), may hold values from 0 to 3
- live_counts: int32 [96], P('grid'), may hold values from 170 to 512, as said below
- observed_value: float32 [49152], P('grid'), may hold values from -5 to 5
- error_variance: float32 [49152], P('grid'), may hold values from 2 to 32
Outputs:
- analysis: float32 [128, 4, 96, 1440], P('mem', None, 'grid')
The draws below stay inside these ranges and needn't reach their ends.
Inputs may be any that keep to these rules, and one draw needn't show every extreme that they name: `live_counts`: slots of a block at or past its count are not observations; some block has all 512 slots live and some block exactly 170. `observed_cell`: a cell is its latitude row within the block times 1440 plus its longitude.
All inputs are finite; a program needn't handle non-finite values. No bound on the sum of `sea_mask` on one device may be relied on, other than what follows from the above.
Results may differ from the reference program's by a relative error of at most 0.000071.
Values sent between devices are 32-bit elements; how exact they have to be, the bound alone decides.
A program may use at most 32 MiB of HBM per device.

```python
import math
import jax
import jax.numpy as jnp
from jax import lax

LON = 1440
LAT_DEV = 1
LEV = 4
OBS_DEV = 512
STEPS = 4
ENS = 128
LAT = 96
OBS = 49152
N_GRID = 96


def draw_live_counts(key, part):
    key_counts, key_order = jax.random.split(key)
    counts = jax.random.randint(key_counts, (N_GRID,), OBS_DEV // 3, OBS_DEV + 1)
    order = jax.random.permutation(key_order, N_GRID)
    counts = counts.at[order[0]].set(OBS_DEV).at[order[1]].set(OBS_DEV // 3)
    return counts.astype(jnp.int32)


def set_ends(result, rng, smallest, top_value):
    longest = result.shape.index(max(result.shape))
    spots = []
    for shift in (0, 1):
        where = [jax.random.randint(jax.random.fold_in(rng, axis), (), 0, length) for axis, length in enumerate(result.shape)]
        where[longest] = (where[longest] + shift) % result.shape[longest]
        spots.append(tuple(where))
    return result.at[spots[0]].set(smallest).at[spots[1]].set(top_value)


def steps_of(rng, extent, pieces, smallest, largest):
    loudness, own = 1.0, jax.random.fold_in(rng, 6)
    for axis_at, shards_of in pieces:
        heights = jnp.exp(jax.random.uniform(jax.random.fold_in(own, axis_at), (shards_of,), jnp.float32, smallest / len(pieces), largest / len(pieces)))
        loudness = loudness * jnp.repeat(heights, extent[axis_at] // shards_of).reshape([-1 if axis == axis_at else 1 for axis in range(len(extent))])
    return loudness


def normal_values(rng, shape, scale, most, cuts=(), kind=jnp.bfloat16):
    loudness = steps_of(rng, shape, cuts, -0.22, 0.18) if cuts else 1.0
    array = jax.random.normal(rng, shape, jnp.float32) * scale * loudness
    return jnp.minimum(jnp.maximum(array, -most), most).astype(kind)


def setup_inputs(seed: int = 0) -> dict:
    arg_keys = jax.random.split(jax.random.key(seed), 10)
    return {
        "background_elapsed_years": normal_values(arg_keys[0], (ENS, LEV, LAT, LON), 1.0, 6.0, ((0, 8), (2, 96)), jnp.float32),
        "currents": jnp.clip(jax.random.uniform(arg_keys[1], (2, LEV, LAT, LON), jnp.float32, -0.1, 0.1) * steps_of(arg_keys[1], (2, LEV, LAT, LON), ((2, 96),), -0.4, 0.0), -0.1, 0.1),
        "diffusivity": jnp.clip(jnp.exp(math.log(0.1) - 2.3025851 * jax.random.uniform(arg_keys[2], (LEV, LAT, LON), jnp.float32) ** steps_of(arg_keys[2], (LEV, LAT, LON), ((1, 96),), -0.2, 0.2)), 0.01, 0.1),
        "sea_mask": set_ends((jax.random.randint(arg_keys[3], (LAT, LON), 0, 8) < 7).astype(jnp.int32), jax.random.fold_in(arg_keys[3], 1), 0, 1),
        "observed_cell": set_ends(jax.random.randint(arg_keys[4], (OBS,), 0, LAT_DEV * LON), jax.random.fold_in(arg_keys[4], 1), 0, (LAT_DEV * LON) - 1).astype(jnp.int32),
        "measured_layer_number": set_ends(jax.random.randint(arg_keys[5], (OBS,), 0, LEV), jax.random.fold_in(arg_keys[5], 1), 0, LEV - 1).astype(jnp.int32),
        "live_counts": draw_live_counts(jax.random.fold_in(arg_keys[9], 71), 0),
        "observed_value": normal_values(arg_keys[7], (OBS,), 1.0, 5.0, ((0, 96),), jnp.float32),
        "error_variance": jnp.clip(jnp.exp(math.log(32.0) - 2.7725887 * jax.random.uniform(arg_keys[8], (OBS,), jnp.float32) ** steps_of(arg_keys[8], (OBS,), ((0, 96),), -0.2, 0.2)), 2.0, 32.0),
    }


VERTICAL_MIX = 0.05
AGE_RATE = 0.25
SURFACE_RELAX = 0.5
HIGHEST = lax.Precision.HIGHEST

def advance(state, padded, zonal_speed, kappa, north_speed, padded_kappa, sea_float, padded_sea):
    east_speed = 0.5 * (zonal_speed + jnp.roll(zonal_speed, -1, -1))
    east_kappa = 0.5 * (kappa + jnp.roll(kappa, -1, -1))
    east_open = sea_float * jnp.roll(sea_float, -1, -1)
    east_value = jnp.roll(state, -1, -1)
    zonal_flux = east_open * (jnp.maximum(east_speed, 0.0) * state + jnp.minimum(east_speed, 0.0) * east_value - east_kappa * (east_value - state))
    face_speed = 0.5 * (north_speed[..., :-1, :] + north_speed[..., 1:, :])
    face_kappa = 0.5 * (padded_kappa[..., :-1, :] + padded_kappa[..., 1:, :])
    face_open = padded_sea[:-1] * padded_sea[1:]
    below_rows = padded[..., :-1, :]
    above_rows = padded[..., 1:, :]
    north_flux = face_open * (jnp.maximum(face_speed, 0.0) * below_rows + jnp.minimum(face_speed, 0.0) * above_rows - face_kappa * (above_rows - below_rows))
    change = -(zonal_flux - jnp.roll(zonal_flux, 1, -1)) - (north_flux[..., 1:, :] - north_flux[..., :-1, :])
    vertical = VERTICAL_MIX * sea_float * (state[..., 1:, :, :] - state[..., :-1, :, :])
    zero_layer = jnp.zeros_like(state[..., :1, :, :])
    change = change + jnp.concatenate([vertical, zero_layer], -3) - jnp.concatenate([zero_layer, vertical], -3)
    stepped = state + change + AGE_RATE * sea_float
    surface = stepped[..., :1, :, :] * (1.0 - SURFACE_RELAX * sea_float)
    return jnp.concatenate([surface, stepped[..., 1:, :, :]], -3)

def projection(running_number):
    row_index = jnp.arange(running_number)[:, None]
    column_index = jnp.arange(running_number - 1)[None, :]
    count_root = math.sqrt(running_number)
    interior = (row_index == column_index).astype(jnp.float32) - 1.0 / (running_number * (1.0 / count_root + 1.0))
    return jnp.where(row_index == running_number - 1, -1.0 / count_root, interior).astype(jnp.float32)

def stacked_rows(globally_measured, observed_value, error_variance, live_slot, projector):
    running_number = globally_measured.shape[0]
    member_mean = lax.optimization_barrier(jnp.sum(globally_measured, 0)) / running_number
    innovation = observed_value - member_mean
    scaled = jnp.where(live_slot, 1.0 / jnp.sqrt(error_variance), 0.0)
    projected = jnp.dot(projector.T, globally_measured, precision=HIGHEST)
    return jnp.concatenate([projected, innovation[None, :]], 0) * scaled[None, :]

def mixing_matrix(triangle, projector):
    running_number = triangle.shape[0]
    leading = triangle[:running_number - 1, :running_number - 1]
    carry_q = triangle[:running_number - 1, running_number - 1]
    identity = jnp.eye(running_number - 1, dtype=triangle.dtype)
    inverse = lax.linalg.triangular_solve(leading, identity, left_side=True, lower=False)
    weights = jnp.dot(inverse, carry_q, precision=HIGHEST)
    spread = math.sqrt(running_number - 1) * jnp.dot(jnp.dot(projector, inverse, precision=HIGHEST), projector.T, precision=HIGHEST)
    return 1.0 / running_number + jnp.dot(projector, weights, precision=HIGHEST)[:, None] + spread

def pad_rows(field):
    widths = [(0, 0)] * (field.ndim - 2) + [(1, 1), (0, 0)]
    return jnp.pad(field, widths)

def reference(background_elapsed_years, currents, diffusivity, sea_mask, observed_cell, measured_layer_number, live_counts, observed_value, error_variance):
    sea_float = sea_mask.astype(jnp.float32)
    north_speed = pad_rows(currents[1])
    padded_kappa = pad_rows(diffusivity)
    padded_sea = pad_rows(sea_float)

    def ensemble_position(state):
        for step_index in range(STEPS):
            state = advance(state, pad_rows(state), currents[0], diffusivity, north_speed, padded_kappa, sea_float, padded_sea)
        return state
    predicted_state_grid = lax.map(ensemble_position, background_elapsed_years)
    slot_index = jnp.arange(OBS).astype(jnp.int32)
    block_index = slot_index // OBS_DEV
    meridional_position = block_index * LAT_DEV + observed_cell // LON
    easting_position = observed_cell % LON
    globally_measured = predicted_state_grid[:, measured_layer_number, meridional_position, easting_position]
    live_slot = slot_index % OBS_DEV < live_counts[block_index]
    running_number = globally_measured.shape[0]
    projector = projection(running_number)
    stacked = stacked_rows(globally_measured, observed_value, error_variance, live_slot, projector)
    gram_total = jnp.dot(stacked, stacked.T, precision=HIGHEST) + (running_number - 1) * jnp.eye(running_number, dtype=jnp.float32)
    triangle = jnp.linalg.cholesky(gram_total).T
    mixing = mixing_matrix(triangle, projector)
    unrolled_array = predicted_state_grid.reshape(running_number, -1)
    return jnp.dot(mixing.T, unrolled_array, precision=HIGHEST).reshape(background_elapsed_years.shape)
```

```python
import functools
import math

import jax
import jax.numpy as jnp
from jax import lax
from jax.experimental import pallas as pl
from jax.experimental.pallas import tpu as pltpu
from jax.sharding import PartitionSpec as P

STEPS = 4
Z_RING = 12
LANES = 128
PANEL = 32
VERTICAL_MIX = 0.05
AGE_RATE = 0.25
SURFACE_RELAX = 0.5
HIGHEST = lax.Precision.HIGHEST
MESH = pl.DeviceIdType.MESH


def faces(speed_a, speed_b, kappa_a, kappa_b, sea_a, sea_b):
    speed = 0.5 * (speed_a + speed_b)
    kappa = 0.5 * (kappa_a + kappa_b)
    both = sea_a * sea_b
    return both * (jnp.maximum(speed, 0.0) + kappa), both * (jnp.minimum(speed, 0.0) - kappa)


def factor_inverse(gram, count):
    lane = lax.broadcasted_iota(jnp.int32, (PANEL, count), 1)
    row = lax.broadcasted_iota(jnp.int32, (PANEL, 1), 0)
    wide_row = lax.broadcasted_iota(jnp.int32, (PANEL, count), 0)
    full_row = lax.broadcasted_iota(jnp.int32, (count, count), 0)
    full_lane = lax.broadcasted_iota(jnp.int32, (count, count), 1)
    left = gram + jnp.where(full_row == full_lane, float(count - 1), 0.0)
    right = jnp.where(full_row == full_lane, 1.0, 0.0)
    done = []
    for first in range(0, count, PANEL):
        a, e = left[:PANEL], right[:PANEL]
        for k in range(PANEL):
            at = first + k
            scale = 1.0 / a[k : k + 1, at : at + 1]
            factor = jnp.where(row > k, a[:, at : at + 1] * scale, 0.0)
            a = a - factor * a[k : k + 1]
            e = e - factor * e[k : k + 1]
        pivots = jnp.sum(jnp.where(lane == wide_row + first, a, 0.0), axis=1, keepdims=True)
        root = lax.rsqrt(pivots)
        a, e = a * root, e * root
        done.append(e)
        if first + PANEL < count:
            turned = jnp.transpose(a)[first + PANEL :]
            left = left[PANEL:] - jnp.dot(turned, a, precision=HIGHEST)
            right = right[PANEL:] - jnp.dot(turned, e, precision=HIGHEST)
    return jnp.concatenate(done, 0)


def kernel(
    cfg,
    state_ref, vk_ref, us_ref, sea_ref, cell_ref, level_ref, live_ref, value_ref, variance_ref,
    out_ref,
    states, from_south, from_north, vk_south, vk_north, sea_south, sea_north,
    coefs, units, own_all, picks, part, slice_parts, z_own, z_parts, y_own, y_parts, total, gram, mixed,
    s_halo, r_halo, s_static, r_static, s_out, r_out, s_slice, r_slice, s_z, r_z, s_y, r_y, s_all, r_all, s_back, r_back,
):
    n_grid, n_mem, z_ring, levels, wide, chunks = cfg
    y_ring = n_grid // z_ring
    own = 8 * chunks
    count = n_mem * own
    unit_wide = levels * wide // n_mem
    halves = n_mem // levels
    grid = lax.axis_index("grid")
    mem = lax.axis_index("mem")
    y_at, z_at = grid // z_ring, lax.rem(grid, z_ring)
    has_north, has_south = grid < n_grid - 1, grid > 0

    def mem_peer(d):
        return lax.rem(mem + d, n_mem)

    def z_peer(d):
        return y_at * z_ring + lax.rem(z_at + d, z_ring)

    def y_peer(d):
        return lax.rem(y_at + d, y_ring) * z_ring + z_at

    barrier = pltpu.get_barrier_semaphore()

    def greet(where):
        pl.semaphore_signal(barrier, inc=1, device_id=where, device_id_type=MESH)

    cross_north = jnp.logical_and(has_north, z_at == z_ring - 1)
    cross_south = jnp.logical_and(has_south, z_at == 0)

    @pl.when(cross_north)
    def _():
        greet({"grid": grid + 1})

    @pl.when(cross_south)
    def _():
        greet({"grid": grid - 1})

    for d in range(1, z_ring):
        greet({"grid": z_peer(d)})
    for d in range(1, y_ring):
        greet({"grid": y_peer(d)})
    for d in range(1, n_mem):
        greet({"mem": mem_peer(d)})
    greeted = z_ring + y_ring + n_mem - 3 + cross_north.astype(jnp.int32) + cross_south.astype(jnp.int32)
    pl.semaphore_wait(barrier, greeted)

    def remote(src, dst, send, recv, where):
        return pltpu.make_async_remote_copy(
            src_ref=src, dst_ref=dst, send_sem=send, recv_sem=recv, device_id=where, device_id_type=MESH
        )

    north, south = {"grid": grid + 1}, {"grid": grid - 1}

    def halo(step, chunk):
        src = state_ref.at[chunk] if step == 0 else states.at[step - 1, chunk]
        up = remote(src, from_south.at[step, chunk], s_halo.at[0, step, chunk], r_halo.at[0, step, chunk], north)
        down = remote(src, from_north.at[step, chunk], s_halo.at[1, step, chunk], r_halo.at[1, step, chunk], south)
        return up, down

    static_up = (
        remote(vk_ref, vk_south, s_static.at[0, 0], r_static.at[0, 0], north),
        remote(sea_ref, sea_south, s_static.at[0, 1], r_static.at[0, 1], north),
    )
    static_down = (
        remote(vk_ref, vk_north, s_static.at[1, 0], r_static.at[1, 0], south),
        remote(sea_ref, sea_north, s_static.at[1, 1], r_static.at[1, 1], south),
    )

    def start_halo(step, chunk):
        up, down = halo(step, chunk)
        pl.when(has_north)(up.start)
        pl.when(has_south)(down.start)

    for copy in static_up:
        pl.when(has_north)(copy.start)
    for copy in static_down:
        pl.when(has_south)(copy.start)
    for chunk in range(chunks):
        start_halo(0, chunk)

    @pl.when(jnp.logical_not(has_south))
    def _():
        vk_south[...] = jnp.zeros_like(vk_south)
        sea_south[...] = jnp.zeros_like(sea_south)
        from_south[...] = jnp.zeros_like(from_south)

    @pl.when(jnp.logical_not(has_north))
    def _():
        vk_north[...] = jnp.zeros_like(vk_north)
        sea_north[...] = jnp.zeros_like(sea_north)
        from_north[...] = jnp.zeros_like(from_north)

    slots = cell_ref.shape[1]
    place = level_ref[...] * wide + cell_ref[...] - mem * unit_wide
    inside = jnp.logical_and(place >= 0, place < unit_wide)
    live = lax.broadcasted_iota(jnp.int32, (1, slots), 1) < live_ref[...]
    weight = jnp.where(jnp.logical_and(inside, live), 1.0 / jnp.sqrt(variance_ref[...]), 0.0)
    picks[...] = jnp.where(
        lax.broadcasted_iota(jnp.int32, (unit_wide, slots), 0) == place, 1.0, 0.0
    ).astype(jnp.bfloat16)

    velocity, kappa = vk_ref[0:levels], vk_ref[levels : 2 * levels]
    zonal = us_ref[0:levels]
    sea = jnp.broadcast_to(sea_ref[...], (levels, wide))
    a_east, b_east = faces(
        zonal, pltpu.roll(zonal, wide - 1, 1), kappa, pltpu.roll(kappa, wide - 1, 1), sea, pltpu.roll(sea, wide - 1, 1)
    )
    a_west, b_west = pltpu.roll(a_east, 1, 1), pltpu.roll(b_east, 1, 1)

    for copy in static_up:
        pl.when(has_south)(copy.wait_recv)
    for copy in static_down:
        pl.when(has_north)(copy.wait_recv)
    a_north, b_north = faces(
        velocity, vk_north[0:levels], kappa, vk_north[levels : 2 * levels], sea,
        jnp.broadcast_to(sea_north[...], (levels, wide)),
    )
    a_south, b_south = faces(
        vk_south[0:levels], velocity, vk_south[levels : 2 * levels], kappa,
        jnp.broadcast_to(sea_south[...], (levels, wide)), sea,
    )
    depth = lax.broadcasted_iota(jnp.int32, (levels, wide), 0)
    vertical = VERTICAL_MIX * sea
    borders = jnp.where(jnp.logical_or(depth == 0, depth == levels - 1), 1.0, 2.0)
    relax = jnp.where(depth == 0, 1.0 - SURFACE_RELAX * sea, 1.0)
    centre = 1.0 - a_east + b_west - a_north + b_south - borders * vertical
    parts = (centre, -b_east, a_west, -b_north, a_south, vertical, AGE_RATE * sea)
    for index, values in enumerate(parts):
        values = values * relax
        for level in range(levels):
            coefs[level, index] = jnp.broadcast_to(values[level : level + 1], (8, wide))

    for step in range(STEPS):
        for chunk in range(chunks):
            up, down = halo(step, chunk)
            pl.when(has_south)(up.wait_recv)
            pl.when(has_north)(down.wait_recv)
            for level in range(levels):
                def at(which):
                    return state_ref[chunk, which] if step == 0 else states[step - 1, chunk, which]

                here = at(level)
                around = at(level - 1) if level > 0 else 0.0
                if level < levels - 1:
                    around = around + at(level + 1)
                result = (
                    coefs[level, 0] * here
                    + coefs[level, 1] * pltpu.roll(here, wide - 1, 1)
                    + coefs[level, 2] * pltpu.roll(here, 1, 1)
                    + coefs[level, 3] * from_north[step, chunk, level]
                    + coefs[level, 4] * from_south[step, chunk, level]
                    + coefs[level, 5] * around
                    + coefs[level, 6]
                )
                if step < STEPS - 1:
                    states[step, chunk, level] = result
                else:
                    for half in range(halves):
                        units[level * halves + half, chunk] = result[:, half * unit_wide : (half + 1) * unit_wide]
            if step < STEPS - 1:
                start_halo(step + 1, chunk)
            else:
                rows = pl.ds(pl.multiple_of(mem * own + 8 * chunk, 8), 8)
                for d in range(1, n_mem):
                    remote(
                        units.at[mem_peer(d), chunk], own_all.at[rows], s_out.at[d - 1, chunk], r_out.at[d - 1, chunk],
                        {"mem": mem_peer(d)},
                    ).start()
                own_all[rows, :] = units[mem, chunk]

    def exchange(src_of, dst_of, send, recv, peers, axis, peer):
        return [remote(src_of(d), dst_of(d), send.at[d - 1], recv.at[d - 1], {axis: peer(d)}) for d in range(1, peers)]

    outs = [
        remote(
            units.at[mem_peer(d), chunk],
            own_all.at[pl.ds(pl.multiple_of(mem * own + 8 * chunk, 8), 8)],
            s_out.at[d - 1, chunk], r_out.at[d - 1, chunk], {"mem": mem_peer(d)},
        )
        for d in range(1, n_mem)
        for chunk in range(chunks)
    ]
    for copy in outs:
        copy.wait_recv()

    fields = own_all[...]
    high = fields.astype(jnp.bfloat16)
    rest = fields - high.astype(jnp.float32)
    middle = rest.astype(jnp.bfloat16)
    low = (rest - middle.astype(jnp.float32)).astype(jnp.bfloat16)
    seen = (
        jnp.dot(high, picks[...], preferred_element_type=jnp.float32)
        + jnp.dot(middle, picks[...], preferred_element_type=jnp.float32)
        + jnp.dot(low, picks[...], preferred_element_type=jnp.float32)
    )
    root = math.sqrt(count)
    inner = 1.0 / (count * (1.0 / root + 1.0))
    last = lax.broadcasted_iota(jnp.int32, (count, slots), 0) == count - 1
    everyone = jnp.sum(seen, axis=0, keepdims=True)
    final = seen[count - 1 : count]
    shared = -inner * (everyone - final) - final / root
    stacked = jnp.where(last, value_ref[...] - everyone / count, seen + shared) * weight
    part[...] = lax.dot_general(
        stacked, stacked, (((1,), (1,)), ((), ())), precision=HIGHEST, preferred_element_type=jnp.float32
    ).reshape(n_mem, own, count)

    slices = exchange(lambda d: part.at[mem_peer(d)], lambda d: slice_parts.at[d - 1], s_slice, r_slice, n_mem, "mem", mem_peer)
    for copy in slices:
        copy.start()
    for copy in slices:
        copy.wait_recv()
    z_own[...] = part[mem] + jnp.sum(slice_parts[...], axis=0)
    along_z = exchange(lambda d: z_own, lambda d: z_parts.at[d - 1], s_z, r_z, z_ring, "grid", z_peer)
    for copy in along_z:
        copy.start()
    for copy in along_z:
        copy.wait_recv()
    y_own[...] = z_own[...] + jnp.sum(z_parts[...], axis=0)
    along_y = exchange(lambda d: y_own, lambda d: y_parts.at[d - 1], s_y, r_y, y_ring, "grid", y_peer)
    for copy in along_y:
        copy.start()
    for copy in along_y:
        copy.wait_recv()
    total[...] = y_own[...] + jnp.sum(y_parts[...], axis=0)
    gathered = exchange(lambda d: total, lambda d: gram.at[mem], s_all, r_all, n_mem, "mem", mem_peer)
    for copy in gathered:
        copy.start()
    gram[mem] = total[...]
    for copy in gathered:
        copy.wait_recv()

    inverse = factor_inverse(gram[...].reshape(count, count), count)
    square_lane = lax.broadcasted_iota(jnp.int32, (count, count), 1)
    square_row = lax.broadcasted_iota(jnp.int32, (count, count), 0)
    leading = jnp.where(square_lane < count - 1, inverse, 0.0)
    across = jnp.sum(leading, axis=1, keepdims=True)
    turned = jnp.where(square_lane == count - 1, -across / root, leading - inner * across)
    shift = -turned[count - 1 : count] / inverse[count - 1 : count, count - 1 : count]
    kept = jnp.where(square_row < count - 1, turned, 0.0)
    down_sum = jnp.sum(kept, axis=0, keepdims=True)
    spread = jnp.where(square_row == count - 1, -down_sum / root, kept - inner * down_sum)
    mixing = 1.0 / count + shift + math.sqrt(count - 1) * spread
    mixed[...] = jnp.dot(mixing, own_all[...], precision=HIGHEST).reshape(n_mem, own, unit_wide)
    back = exchange(lambda d: mixed.at[mem_peer(d)], lambda d: out_ref.at[mem], s_back, r_back, n_mem, "mem", mem_peer)
    for copy in back:
        copy.start()
    out_ref[mem] = mixed[mem]
    for copy in back:
        copy.wait_recv()

    for step in range(STEPS):
        for chunk in range(chunks):
            up, down = halo(step, chunk)
            pl.when(has_north)(up.wait_send)
            pl.when(has_south)(down.wait_send)
    for copy in static_up:
        pl.when(has_north)(copy.wait_send)
    for copy in static_down:
        pl.when(has_south)(copy.wait_send)
    for copy in outs + slices + along_z + along_y + gathered + back:
        copy.wait_send()


def ring(x, wide):
    lon = x.shape[-1]
    gap = jnp.zeros(x.shape[:-1] + (wide - lon - 2 * STEPS,), x.dtype)
    return jnp.concatenate([x, x[..., :STEPS], gap, x[..., lon - STEPS :]], -1)


def per_device(
    n_grid, n_mem, z_ring,
    background_elapsed_years, currents, diffusivity, sea_mask, observed_cell, measured_layer_number, live_counts,
    observed_value, error_variance,
):
    own, levels, _, lon = background_elapsed_years.shape
    chunks, slots = own // 8, observed_cell.shape[0]
    halves = n_mem // levels
    block = LANES * halves
    wide = -(-(lon + 2 * STEPS) // block) * block
    unit_wide = wide // halves
    y_ring = n_grid // z_ring
    count = own * n_mem
    state = ring(background_elapsed_years.reshape(chunks, 8, levels, lon).transpose(0, 2, 1, 3), wide)
    vk = ring(jnp.concatenate([currents[1, :, 0], diffusivity[:, 0]], 0), wide)
    us = ring(currents[0, :, 0], wide)
    sea = ring(sea_mask.astype(jnp.float32), wide)
    f32 = jnp.float32
    dma = pltpu.SemaphoreType.DMA
    halo_shape = (STEPS, chunks, levels, 8, wide)
    scratch = [
        pltpu.VMEM((STEPS - 1, chunks, levels, 8, wide), f32),
        pltpu.VMEM(halo_shape, f32),
        pltpu.VMEM(halo_shape, f32),
        pltpu.VMEM((2 * levels, wide), f32),
        pltpu.VMEM((2 * levels, wide), f32),
        pltpu.VMEM((1, wide), f32),
        pltpu.VMEM((1, wide), f32),
        pltpu.VMEM((levels, 7, 8, wide), f32),
        pltpu.VMEM((n_mem, chunks, 8, unit_wide), f32),
        pltpu.VMEM((count, unit_wide), f32),
        pltpu.VMEM((unit_wide, slots), jnp.bfloat16),
        pltpu.VMEM((n_mem, own, count), f32),
        pltpu.VMEM((n_mem - 1, own, count), f32),
        pltpu.VMEM((own, count), f32),
        pltpu.VMEM((z_ring - 1, own, count), f32),
        pltpu.VMEM((own, count), f32),
        pltpu.VMEM((y_ring - 1, own, count), f32),
        pltpu.VMEM((own, count), f32),
        pltpu.VMEM((n_mem, own, count), f32),
        pltpu.VMEM((n_mem, own, unit_wide), f32),
    ]
    semaphores = [
        dma((2, STEPS, chunks)), dma((2, STEPS, chunks)),
        dma((2, 2)), dma((2, 2)),
        dma((n_mem - 1, chunks)), dma((n_mem - 1, chunks)),
        dma((n_mem - 1,)), dma((n_mem - 1,)),
        dma((z_ring - 1,)), dma((z_ring - 1,)),
        dma((y_ring - 1,)), dma((y_ring - 1,)),
        dma((n_mem - 1,)), dma((n_mem - 1,)),
        dma((n_mem - 1,)), dma((n_mem - 1,)),
    ]
    vmem = pl.BlockSpec(memory_space=pltpu.VMEM)
    result = pl.pallas_call(
        functools.partial(kernel, (n_grid, n_mem, z_ring, levels, wide, chunks)),
        out_shape=jax.ShapeDtypeStruct((n_mem, own, unit_wide), f32),
        in_specs=[vmem] * 9,
        out_specs=vmem,
        scratch_shapes=scratch + semaphores,
        compiler_params=pltpu.CompilerParams(
            collective_id=0, has_side_effects=True, vmem_limit_bytes=40 * 1024 * 1024
        ),
    )(
        state, vk, us, sea, observed_cell[None], measured_layer_number[None], live_counts[None],
        observed_value[None], error_variance[None],
    )
    whole = result.reshape(levels, halves, own, unit_wide).transpose(2, 0, 1, 3).reshape(own, levels, wide)
    return whole[:, :, None, :lon]


def solution(mesh):
    placed = (
        P("mem", None, "grid", None),
        P(None, None, "grid", None),
        P(None, "grid", None),
        P("grid", None),
        P("grid"),
        P("grid"),
        P("grid"),
        P("grid"),
        P("grid"),
    )
    return jax.shard_map(
        functools.partial(per_device, mesh.shape["grid"], mesh.shape["mem"], Z_RING),
        mesh=mesh,
        in_specs=placed,
        out_specs=P("mem", None, "grid", None),
        check_vma=False,
    )
```

```python
import functools
import math

import jax
import jax.numpy as jnp
from jax import lax
from jax.experimental import pallas as pl
from jax.experimental.pallas import tpu as pltpu
from jax.sharding import PartitionSpec as P

STEPS = 4
Z_RING = 12
LANES = 128
PANEL = 64
VERTICAL_MIX = 0.05
AGE_RATE = 0.25
SURFACE_RELAX = 0.5
HIGHEST = lax.Precision.HIGHEST
MESH = pl.DeviceIdType.MESH


def faces(speed_a, speed_b, kappa_a, kappa_b, sea_a, sea_b):
    speed = 0.5 * (speed_a + speed_b)
    kappa = 0.5 * (kappa_a + kappa_b)
    both = sea_a * sea_b
    return both * (jnp.maximum(speed, 0.0) + kappa), both * (jnp.minimum(speed, 0.0) - kappa)


def factor_inverse(gram, count):
    panel = min(PANEL, count)
    wide_row = lax.broadcasted_iota(jnp.int32, (panel, count), 0)
    lane = lax.broadcasted_iota(jnp.int32, (panel, count), 1)
    row = lax.broadcasted_iota(jnp.int32, (8, count), 0)
    full_row = lax.broadcasted_iota(jnp.int32, (count, count), 0)
    full_lane = lax.broadcasted_iota(jnp.int32, (count, count), 1)
    left = gram + jnp.where(full_row == full_lane, float(count - 1), 0.0)
    right = jnp.where(full_row == full_lane, 1.0, 0.0)
    done = []
    for first in range(0, count, panel):
        a_rest, e_rest = left[:panel], right[:panel]
        a_done, e_done = [], []
        for base in range(first, first + panel, 8):
            a, e, a_rest, e_rest = a_rest[:8], e_rest[:8], a_rest[8:], e_rest[8:]
            columns = [jnp.broadcast_to(a[:, base + j : base + j + 1], (8, count)) for j in range(8)]
            scales = []
            for k in range(0, 8, 2):
                now, later = columns[k], columns[k + 1]
                p, q, r = now[k : k + 1], now[k + 1 : k + 2], later[k + 1 : k + 2]
                per_pair, per_p = 1.0 / (p * r - q * q), 1.0 / p
                below_now, below_later = jnp.where(row > k + 1, now, 0.0), jnp.where(row > k + 1, later, 0.0)
                first_factor = (below_now * r - below_later * q) * per_pair
                later_factor = (below_later * p - below_now * q) * per_pair
                first_factor = jnp.where(row == k + 1, q * per_p, first_factor)
                for j in range(k + 2, 8):
                    at = columns[j]
                    columns[j] = at - (first_factor * at[k : k + 1] + later_factor * at[k + 1 : k + 2])
                a = a - (first_factor * a[k : k + 1] + later_factor * a[k + 1 : k + 2])
                e = e - (first_factor * e[k : k + 1] + later_factor * e[k + 1 : k + 2])
                scales += [per_p, per_pair * p]
            a_done.append(a)
            e_done.append(e)
            rows = first + panel - base - 8
            if rows:
                lower = [jnp.broadcast_to(a_rest[:, base + j : base + j + 1], (rows, count)) for j in range(8)]
                for k in range(8):
                    factor = lower[k] * scales[k]
                    for j in range(k + 1, 8):
                        lower[j] = lower[j] - factor * columns[j][k : k + 1]
                    a_rest = a_rest - factor * a[k : k + 1]
                    e_rest = e_rest - factor * e[k : k + 1]
        a, e = jnp.concatenate(a_done, 0), jnp.concatenate(e_done, 0)
        pivots = jnp.sum(jnp.where(lane == wide_row + first, a, 0.0), axis=1, keepdims=True)
        root = lax.rsqrt(pivots)
        a, e = a * root, e * root
        done.append(e)
        if first + panel < count:
            turned = jnp.transpose(a)[first + panel :]
            left = left[panel:] - jnp.dot(turned, a, precision=HIGHEST)
            right = right[panel:] - jnp.dot(turned, e, precision=HIGHEST)
    return jnp.concatenate(done, 0)


def ring(x, wide):
    rows, lon = x.shape
    gap = jnp.zeros((rows, wide - lon - 2 * STEPS), x.dtype)
    return jnp.concatenate([x, x[:, :STEPS], gap, x[:, lon - STEPS :]], 1)


def kernel(
    cfg,
    first_hbm, currents_hbm, kappa_hbm, mask_hbm, cell_hbm, level_hbm, live_hbm, value_hbm, variance_hbm,
    out_ref,
    first_ref, currents_ref, kappa_ref, mask_ref, cell_ref, level_ref, live_ref, value_ref, variance_ref,
    states, raw_south, raw_north, from_south, from_north, v_south, v_north, k_south, k_north, mask_south, mask_north,
    coefs, units, own_all, picks, part, slice_parts, y_own, y_parts, z_own, z_parts, total, gram, mixed, landed, final_ref,
    s_in, s_halo, r_halo, s_static, r_static, s_out, r_out, s_slice, r_slice, s_z, r_z, s_y, r_y,
    s_all, r_all, s_back, r_back, s_leave,
):
    n_grid, n_mem, z_ring, levels, wide, chunks = cfg
    y_ring = n_grid // z_ring
    own = 8 * chunks
    count = n_mem * own
    unit_wide = levels * wide // n_mem
    halves = n_mem // levels
    grid = lax.axis_index("grid")
    mem = lax.axis_index("mem")
    y_at, z_at = grid // z_ring, lax.rem(grid, z_ring)
    has_north, has_south = grid < n_grid - 1, grid > 0

    def mem_peer(d):
        return lax.rem(mem + d, n_mem)

    def z_peer(d):
        return y_at * z_ring + lax.rem(z_at + d, z_ring)

    def y_peer(d):
        return lax.rem(y_at + d, y_ring) * z_ring + z_at

    local = [
        pltpu.make_async_copy(src, dst, s_in.at[index])
        for index, (src, dst) in enumerate(
            (
                (first_hbm, first_ref), (currents_hbm, currents_ref), (kappa_hbm, kappa_ref), (mask_hbm, mask_ref),
                (cell_hbm, cell_ref), (level_hbm, level_ref), (live_hbm, live_ref), (value_hbm, value_ref),
                (variance_hbm, variance_ref),
            )
        )
    ]
    for copy in local:
        copy.start()
    barrier = pltpu.get_barrier_semaphore()

    def greet(where):
        pl.semaphore_signal(barrier, inc=1, device_id=where, device_id_type=MESH)

    cross_north = jnp.logical_and(has_north, z_at == z_ring - 1)
    cross_south = jnp.logical_and(has_south, z_at == 0)

    @pl.when(cross_north)
    def _():
        greet({"grid": grid + 1})

    @pl.when(cross_south)
    def _():
        greet({"grid": grid - 1})

    for d in sorted(range(1, z_ring), key=lambda d: min(d, z_ring - d)):
        greet({"grid": z_peer(d)})
    for d in range(1, y_ring):
        greet({"grid": y_peer(d)})
    for d in range(1, n_mem):
        greet({"mem": mem_peer(d)})
    greeted = z_ring + y_ring + n_mem - 3 + cross_north.astype(jnp.int32) + cross_south.astype(jnp.int32)
    pl.semaphore_wait(barrier, greeted)

    def remote(src, dst, send, recv, where):
        return pltpu.make_async_remote_copy(
            src_ref=src, dst_ref=dst, send_sem=send, recv_sem=recv, device_id=where, device_id_type=MESH
        )

    north, south = {"grid": grid + 1}, {"grid": grid - 1}

    def halo(step, chunk):
        if step == 0:
            rows = pl.ds(8 * chunk, 8)
            src, below, above = first_hbm.at[rows], raw_south.at[rows], raw_north.at[rows]
        else:
            src, below, above = states.at[step, chunk], from_south.at[step - 1, chunk], from_north.at[step - 1, chunk]
        up = remote(src, below, s_halo.at[0, step, chunk], r_halo.at[0, step, chunk], north)
        down = remote(src, above, s_halo.at[1, step, chunk], r_halo.at[1, step, chunk], south)
        return up, down

    statics = (currents_hbm.at[1], kappa_hbm, mask_hbm)
    static_up = [
        remote(src, dst, s_static.at[0, index], r_static.at[0, index], north)
        for index, (src, dst) in enumerate(zip(statics, (v_south, k_south, mask_south)))
    ]
    static_down = [
        remote(src, dst, s_static.at[1, index], r_static.at[1, index], south)
        for index, (src, dst) in enumerate(zip(statics, (v_north, k_north, mask_north)))
    ]

    def start_halo(step, chunk):
        up, down = halo(step, chunk)
        pl.when(has_north)(up.start)
        pl.when(has_south)(down.start)

    for copy in static_up:
        pl.when(has_north)(copy.start)
    for copy in static_down:
        pl.when(has_south)(copy.start)
    for chunk in range(chunks):
        start_halo(0, chunk)

    @pl.when(jnp.logical_not(has_south))
    def _():
        v_south[...] = jnp.zeros_like(v_south)
        k_south[...] = jnp.zeros_like(k_south)
        mask_south[...] = jnp.zeros_like(mask_south)
        raw_south[...] = jnp.zeros_like(raw_south)
        from_south[...] = jnp.zeros_like(from_south)

    @pl.when(jnp.logical_not(has_north))
    def _():
        v_north[...] = jnp.zeros_like(v_north)
        k_north[...] = jnp.zeros_like(k_north)
        mask_north[...] = jnp.zeros_like(mask_north)
        raw_north[...] = jnp.zeros_like(raw_north)
        from_north[...] = jnp.zeros_like(from_north)

    def first_rows(ref, chunk, level):
        return ring(ref[8 * chunk : 8 * chunk + 8, level, 0, :], wide)

    for copy in local:
        copy.wait()
    for chunk in range(chunks):
        for level in range(levels):
            states[0, chunk, level] = first_rows(first_ref, chunk, level)
    slots = cell_ref.shape[0]
    place = (level_ref[...] * wide + cell_ref[...]).reshape(1, slots) - mem * unit_wide
    inside = jnp.logical_and(place >= 0, place < unit_wide)
    live = lax.broadcasted_iota(jnp.int32, (1, slots), 1) < live_ref[0]
    weight = jnp.where(jnp.logical_and(inside, live), 1.0 / jnp.sqrt(variance_ref[...].reshape(1, slots)), 0.0)
    picks[...] = jnp.where(
        lax.broadcasted_iota(jnp.int32, (unit_wide, slots), 0) == place, 1.0, 0.0
    ).astype(jnp.bfloat16)

    def rows_of(ref):
        return ring(ref[:, 0, :], wide)

    def sea_of(ref):
        return jnp.broadcast_to(ring(ref[...].astype(jnp.float32), wide), (levels, wide))

    zonal, velocity = ring(currents_ref[0, :, 0, :], wide), ring(currents_ref[1, :, 0, :], wide)
    kappa, sea = rows_of(kappa_ref), sea_of(mask_ref)
    a_east, b_east = faces(
        zonal, pltpu.roll(zonal, wide - 1, 1), kappa, pltpu.roll(kappa, wide - 1, 1), sea, pltpu.roll(sea, wide - 1, 1)
    )
    a_west, b_west = pltpu.roll(a_east, 1, 1), pltpu.roll(b_east, 1, 1)

    for copy in static_up:
        pl.when(has_south)(copy.wait_recv)
    for copy in static_down:
        pl.when(has_north)(copy.wait_recv)
    a_north, b_north = faces(velocity, rows_of(v_north), kappa, rows_of(k_north), sea, sea_of(mask_north))
    a_south, b_south = faces(rows_of(v_south), velocity, rows_of(k_south), kappa, sea_of(mask_south), sea)
    depth = lax.broadcasted_iota(jnp.int32, (levels, wide), 0)
    vertical = VERTICAL_MIX * sea
    borders = jnp.where(jnp.logical_or(depth == 0, depth == levels - 1), 1.0, 2.0)
    relax = jnp.where(depth == 0, 1.0 - SURFACE_RELAX * sea, 1.0)
    centre = 1.0 - a_east + b_west - a_north + b_south - borders * vertical
    parts = (centre, -b_east, a_west, -b_north, a_south, vertical, AGE_RATE * sea)
    for index, values in enumerate(parts):
        values = values * relax
        for level in range(levels):
            coefs[level, index] = jnp.broadcast_to(values[level : level + 1], (8, wide))

    for step in range(STEPS):
        for chunk in range(chunks):
            up, down = halo(step, chunk)
            pl.when(has_south)(up.wait_recv)
            pl.when(has_north)(down.wait_recv)
            for level in range(levels):
                def at(which):
                    return states[step, chunk, which]

                if step == 0:
                    above, below = first_rows(raw_north, chunk, level), first_rows(raw_south, chunk, level)
                else:
                    above, below = from_north[step - 1, chunk, level], from_south[step - 1, chunk, level]
                here = at(level)
                around = at(level - 1) if level > 0 else 0.0
                if level < levels - 1:
                    around = around + at(level + 1)
                result = (
                    coefs[level, 0] * here
                    + coefs[level, 1] * pltpu.roll(here, wide - 1, 1)
                    + coefs[level, 2] * pltpu.roll(here, 1, 1)
                    + coefs[level, 3] * above
                    + coefs[level, 4] * below
                    + coefs[level, 5] * around
                    + coefs[level, 6]
                )
                if step < STEPS - 1:
                    states[step + 1, chunk, level] = result
                else:
                    for half in range(halves):
                        units[level * halves + half, chunk] = result[:, half * unit_wide : (half + 1) * unit_wide]
            if step < STEPS - 1:
                start_halo(step + 1, chunk)
            else:
                rows = pl.ds(pl.multiple_of(mem * own + 8 * chunk, 8), 8)
                for d in range(1, n_mem):
                    remote(
                        units.at[mem_peer(d), chunk], own_all.at[rows], s_out.at[d - 1, chunk], r_out.at[d - 1, chunk],
                        {"mem": mem_peer(d)},
                    ).start()
                own_all[rows, :] = units[mem, chunk]

    def exchange(src_of, dst_of, send, recv, peers, axis, peer):
        return [remote(src_of(d), dst_of(d), send.at[d - 1], recv.at[d - 1], {axis: peer(d)}) for d in range(1, peers)]

    outs = [
        remote(
            units.at[mem_peer(d), chunk],
            own_all.at[pl.ds(pl.multiple_of(mem * own + 8 * chunk, 8), 8)],
            s_out.at[d - 1, chunk], r_out.at[d - 1, chunk], {"mem": mem_peer(d)},
        )
        for d in range(1, n_mem)
        for chunk in range(chunks)
    ]
    for copy in outs:
        copy.wait_recv()

    fields = own_all[...]
    high = fields.astype(jnp.bfloat16)
    rest = fields - high.astype(jnp.float32)
    middle = rest.astype(jnp.bfloat16)
    low = (rest - middle.astype(jnp.float32)).astype(jnp.bfloat16)
    seen = (
        jnp.dot(high, picks[...], preferred_element_type=jnp.float32)
        + jnp.dot(middle, picks[...], preferred_element_type=jnp.float32)
        + jnp.dot(low, picks[...], preferred_element_type=jnp.float32)
    )
    root = math.sqrt(count)
    inner = 1.0 / (count * (1.0 / root + 1.0))
    last = lax.broadcasted_iota(jnp.int32, (count, slots), 0) == count - 1
    everyone = jnp.sum(seen, axis=0, keepdims=True)
    final = seen[count - 1 : count]
    shared = -inner * (everyone - final) - final / root
    stacked = jnp.where(last, value_ref[...].reshape(1, slots) - everyone / count, seen + shared) * weight
    part[...] = lax.dot_general(
        stacked, stacked, (((1,), (1,)), ((), ())), precision=HIGHEST, preferred_element_type=jnp.float32
    ).reshape(n_mem, own, count)

    slices = exchange(lambda d: part.at[mem_peer(d)], lambda d: slice_parts.at[d - 1], s_slice, r_slice, n_mem, "mem", mem_peer)
    for copy in slices:
        copy.start()
    for copy in slices:
        copy.wait_recv()
    z_own[...] = part[mem] + jnp.sum(slice_parts[...], axis=0)
    along_z = exchange(lambda d: z_own, lambda d: z_parts.at[d - 1], s_z, r_z, z_ring, "grid", z_peer)
    for copy in along_z:
        copy.start()
    for copy in along_z:
        copy.wait_recv()
    y_own[...] = z_own[...] + jnp.sum(z_parts[...], axis=0)
    along_y = exchange(lambda d: y_own, lambda d: y_parts.at[d - 1], s_y, r_y, y_ring, "grid", y_peer)
    for copy in along_y:
        copy.start()
    for copy in along_y:
        copy.wait_recv()
    total[...] = y_own[...] + jnp.sum(y_parts[...], axis=0)
    gathered = exchange(lambda d: total, lambda d: gram.at[mem], s_all, r_all, n_mem, "mem", mem_peer)
    for copy in gathered:
        copy.start()
    gram[mem] = total[...]
    for copy in gathered:
        copy.wait_recv()

    inverse = factor_inverse(gram[...].reshape(count, count), count)
    square_lane = lax.broadcasted_iota(jnp.int32, (count, count), 1)
    square_row = lax.broadcasted_iota(jnp.int32, (count, count), 0)
    leading = jnp.where(square_lane < count - 1, inverse, 0.0)
    across = jnp.sum(leading, axis=1, keepdims=True)
    turned = jnp.where(square_lane == count - 1, -across / root, leading - inner * across)
    shift = -turned[count - 1 : count] / inverse[count - 1 : count, count - 1 : count]
    kept = jnp.where(square_row < count - 1, turned, 0.0)
    down_sum = jnp.sum(kept, axis=0, keepdims=True)
    spread = jnp.where(square_row == count - 1, -down_sum / root, kept - inner * down_sum)
    mixing = 1.0 / count + shift + math.sqrt(count - 1) * spread
    mixed[...] = jnp.dot(mixing, own_all[...], precision=HIGHEST).reshape(n_mem, own, unit_wide)
    mine = (
        mem // halves,
        slice(None),
        pl.ds(pl.multiple_of(lax.rem(mem, halves) * unit_wide, LANES), unit_wide),
    )
    back = exchange(lambda d: mixed.at[mem_peer(d)], lambda d: landed.at[mine], s_back, r_back, n_mem, "mem", mem_peer)
    for copy in back:
        copy.start()
    landed[mine] = mixed[mem]
    for copy in back:
        copy.wait_recv()
    leaving = []
    for level in range(levels):
        final_ref[level] = landed[level][:, : final_ref.shape[2]]
        leaving.append(pltpu.make_async_copy(final_ref.at[level], out_ref.at[:, level, 0, :], s_leave.at[level]))
        leaving[-1].start()

    for step in range(STEPS):
        for chunk in range(chunks):
            up, down = halo(step, chunk)
            pl.when(has_north)(up.wait_send)
            pl.when(has_south)(down.wait_send)
    for copy in static_up:
        pl.when(has_north)(copy.wait_send)
    for copy in static_down:
        pl.when(has_south)(copy.wait_send)
    for copy in leaving:
        copy.wait()
    for copy in outs + slices + along_z + along_y + gathered + back:
        copy.wait_send()


def per_device(
    n_grid, n_mem, z_ring,
    background_elapsed_years, currents, diffusivity, sea_mask, observed_cell, measured_layer_number, live_counts,
    observed_value, error_variance,
):
    own, levels, _, lon = background_elapsed_years.shape
    chunks, slots = own // 8, observed_cell.shape[0]
    halves = n_mem // levels
    block = LANES * halves
    wide = -(-(lon + 2 * STEPS) // block) * block
    unit_wide = wide // halves
    y_ring = n_grid // z_ring
    count = own * n_mem
    f32 = jnp.float32
    dma = pltpu.SemaphoreType.DMA
    halo_shape = (STEPS, chunks, levels, 8, wide)
    i32 = jnp.int32
    scratch = [
        pltpu.VMEM((own, levels, 1, lon), f32),
        pltpu.VMEM((2, levels, 1, lon), f32),
        pltpu.VMEM((levels, 1, lon), f32),
        pltpu.VMEM((1, lon), i32),
        pltpu.VMEM((slots,), i32),
        pltpu.VMEM((slots,), i32),
        pltpu.SMEM((1,), i32),
        pltpu.VMEM((slots,), f32),
        pltpu.VMEM((slots,), f32),
        pltpu.VMEM(halo_shape, f32),
        pltpu.VMEM((own, levels, 1, lon), f32),
        pltpu.VMEM((own, levels, 1, lon), f32),
        pltpu.VMEM((STEPS - 1,) + halo_shape[1:], f32),
        pltpu.VMEM((STEPS - 1,) + halo_shape[1:], f32),
        pltpu.VMEM((levels, 1, lon), f32),
        pltpu.VMEM((levels, 1, lon), f32),
        pltpu.VMEM((levels, 1, lon), f32),
        pltpu.VMEM((levels, 1, lon), f32),
        pltpu.VMEM((1, lon), i32),
        pltpu.VMEM((1, lon), i32),
        pltpu.VMEM((levels, 7, 8, wide), f32),
        pltpu.VMEM((n_mem, chunks, 8, unit_wide), f32),
        pltpu.VMEM((count, unit_wide), f32),
        pltpu.VMEM((unit_wide, slots), jnp.bfloat16),
        pltpu.VMEM((n_mem, own, count), f32),
        pltpu.VMEM((n_mem - 1, own, count), f32),
        pltpu.VMEM((own, count), f32),
        pltpu.VMEM((y_ring - 1, own, count), f32),
        pltpu.VMEM((own, count), f32),
        pltpu.VMEM((z_ring - 1, own, count), f32),
        pltpu.VMEM((own, count), f32),
        pltpu.VMEM((n_mem, own, count), f32),
        pltpu.VMEM((n_mem, own, unit_wide), f32),
        pltpu.VMEM((levels, own, wide), f32),
        pltpu.VMEM((levels, own, lon), f32),
    ]
    semaphores = [
        dma((9,)),
        dma((2, STEPS, chunks)), dma((2, STEPS, chunks)),
        dma((2, 3)), dma((2, 3)),
        dma((n_mem - 1, chunks)), dma((n_mem - 1, chunks)),
        dma((n_mem - 1,)), dma((n_mem - 1,)),
        dma((z_ring - 1,)), dma((z_ring - 1,)),
        dma((y_ring - 1,)), dma((y_ring - 1,)),
        dma((n_mem - 1,)), dma((n_mem - 1,)),
        dma((n_mem - 1,)), dma((n_mem - 1,)),
        dma((levels,)),
    ]
    return pl.pallas_call(
        functools.partial(kernel, (n_grid, n_mem, z_ring, levels, wide, chunks)),
        out_shape=jax.ShapeDtypeStruct((own, levels, 1, lon), f32),
        in_specs=[pl.BlockSpec(memory_space=pltpu.HBM)] * 9,
        out_specs=pl.BlockSpec(memory_space=pltpu.HBM),
        scratch_shapes=scratch + semaphores,
        compiler_params=pltpu.CompilerParams(
            collective_id=0, has_side_effects=True, vmem_limit_bytes=60 * 1024 * 1024
        ),
    )(
        background_elapsed_years, currents, diffusivity, sea_mask, observed_cell, measured_layer_number, live_counts,
        observed_value, error_variance,
    )


def solution(mesh):
    placed = (
        P("mem", None, "grid", None),
        P(None, None, "grid", None),
        P(None, "grid", None),
        P("grid", None),
        P("grid"),
        P("grid"),
        P("grid"),
        P("grid"),
        P("grid"),
    )
    return jax.shard_map(
        functools.partial(per_device, mesh.shape["grid"], mesh.shape["mem"], Z_RING),
        mesh=mesh,
        in_specs=placed,
        out_specs=P("mem", None, "grid", None),
        check_vma=False,
    )
```

```python
import functools
import math

import jax
import jax.numpy as jnp
from jax import lax
from jax.experimental import pallas as pl
from jax.experimental.pallas import tpu as pltpu
from jax.sharding import PartitionSpec as P

STEPS = 4
Z_RING = 12
LANES = 128
PANEL = 64
VERTICAL_MIX = 0.05
AGE_RATE = 0.25
SURFACE_RELAX = 0.5
HIGHEST = lax.Precision.HIGHEST
MESH = pl.DeviceIdType.MESH


def faces(speed_a, speed_b, kappa_a, kappa_b, sea_a, sea_b):
    speed = 0.5 * (speed_a + speed_b)
    kappa = 0.5 * (kappa_a + kappa_b)
    both = sea_a * sea_b
    return both * (jnp.maximum(speed, 0.0) + kappa), both * (jnp.minimum(speed, 0.0) - kappa)


def factor_inverse(gram, count):
    panel = min(PANEL, count)
    wide_row = lax.broadcasted_iota(jnp.int32, (panel, count), 0)
    lane = lax.broadcasted_iota(jnp.int32, (panel, count), 1)
    row = lax.broadcasted_iota(jnp.int32, (8, count), 0)
    full_row = lax.broadcasted_iota(jnp.int32, (count, count), 0)
    full_lane = lax.broadcasted_iota(jnp.int32, (count, count), 1)
    left = gram + jnp.where(full_row == full_lane, float(count - 1), 0.0)
    right = jnp.where(full_row == full_lane, 1.0, 0.0)
    done = []
    for first in range(0, count, panel):
        a_rest, e_rest = left[:panel], right[:panel]
        a_done, e_done = [], []
        for base in range(first, first + panel, 8):
            a, e, a_rest, e_rest = a_rest[:8], e_rest[:8], a_rest[8:], e_rest[8:]
            columns = [jnp.broadcast_to(a[:, base + j : base + j + 1], (8, count)) for j in range(8)]
            scales = []
            for k in range(0, 8, 2):
                now, later = columns[k], columns[k + 1]
                p, q, r = now[k : k + 1], now[k + 1 : k + 2], later[k + 1 : k + 2]
                per_pair, per_p = 1.0 / (p * r - q * q), 1.0 / p
                below_now, below_later = jnp.where(row > k + 1, now, 0.0), jnp.where(row > k + 1, later, 0.0)
                first_factor = (below_now * r - below_later * q) * per_pair
                later_factor = (below_later * p - below_now * q) * per_pair
                first_factor = jnp.where(row == k + 1, q * per_p, first_factor)
                for j in range(k + 2, 8):
                    at = columns[j]
                    columns[j] = at - (first_factor * at[k : k + 1] + later_factor * at[k + 1 : k + 2])
                a = a - (first_factor * a[k : k + 1] + later_factor * a[k + 1 : k + 2])
                e = e - (first_factor * e[k : k + 1] + later_factor * e[k + 1 : k + 2])
                scales += [per_p, per_pair * p]
            a_done.append(a)
            e_done.append(e)
            rows = first + panel - base - 8
            if rows:
                lower = [jnp.broadcast_to(a_rest[:, base + j : base + j + 1], (rows, count)) for j in range(8)]
                for k in range(8):
                    factor = lower[k] * scales[k]
                    for j in range(k + 1, 8):
                        lower[j] = lower[j] - factor * columns[j][k : k + 1]
                    a_rest = a_rest - factor * a[k : k + 1]
                    e_rest = e_rest - factor * e[k : k + 1]
        a, e = jnp.concatenate(a_done, 0), jnp.concatenate(e_done, 0)
        pivots = jnp.sum(jnp.where(lane == wide_row + first, a, 0.0), axis=1, keepdims=True)
        root = lax.rsqrt(pivots)
        a, e = a * root, e * root
        done.append(e)
        if first + panel < count:
            turned = jnp.transpose(a)[first + panel :]
            left = left[panel:] - jnp.dot(turned, a, precision=HIGHEST)
            right = right[panel:] - jnp.dot(turned, e, precision=HIGHEST)
    return jnp.concatenate(done, 0)


def spread_row(flat, level, levels, lon, wide):
    full, last = wide - LANES, lon - (wide - LANES)
    body, packed = flat[:, level * full : (level + 1) * full], flat[:, levels * full :]
    lane = lax.broadcasted_iota(jnp.int32, (8, LANES), 1)
    ending = packed if level == 0 else pltpu.roll(packed, LANES - level * last, 1)
    opening, closing = pltpu.roll(body[:, :LANES], last, 1), pltpu.roll(ending, LANES - last, 1)
    tail = jnp.where(lane < last + STEPS, jnp.where(lane < last, ending, opening), 0.0)
    return jnp.concatenate([body, jnp.where(lane >= LANES - STEPS, closing, tail)], 1)


def ring(x, wide):
    rows, lon = x.shape
    gap = jnp.zeros((rows, wide - lon - 2 * STEPS), x.dtype)
    return jnp.concatenate([x, x[:, :STEPS], gap, x[:, lon - STEPS :]], 1)


def kernel(
    cfg,
    first_hbm, currents_hbm, kappa_hbm, mask_hbm, cell_hbm, level_hbm, live_hbm, value_hbm, variance_hbm,
    out_ref,
    first_ref, currents_ref, kappa_ref, mask_ref, cell_ref, level_ref, live_ref, value_ref, variance_ref,
    states, leaving, raw_south, raw_north, from_south, from_north, v_south, v_north, k_south, k_north, mask_south, mask_north,
    coefs, units, own_all, picks, part, slice_parts, y_own, y_parts, z_own, z_parts, total, gram, mixed, landed,
    s_in, s_halo, r_halo, s_static, r_static, s_out, r_out, s_slice, r_slice, s_z, r_z, s_y, r_y,
    s_all, r_all, s_back, r_back,
):
    n_grid, n_mem, z_ring, levels, lon, wide, chunks = cfg
    y_ring = n_grid // z_ring
    own = 8 * chunks
    count = n_mem * own
    unit_wide = levels * wide // n_mem
    halves = n_mem // levels
    grid = lax.axis_index("grid")
    mem = lax.axis_index("mem")
    y_at, z_at = grid // z_ring, lax.rem(grid, z_ring)
    has_north, has_south = grid < n_grid - 1, grid > 0

    def mem_peer(d):
        return lax.rem(mem + d, n_mem)

    def z_peer(d):
        return y_at * z_ring + lax.rem(z_at + d, z_ring)

    def y_peer(d):
        return lax.rem(y_at + d, y_ring) * z_ring + z_at

    local = [
        pltpu.make_async_copy(src, dst, s_in.at[index])
        for index, (src, dst) in enumerate(
            (
                (first_hbm, first_ref), (currents_hbm, currents_ref), (kappa_hbm, kappa_ref), (mask_hbm, mask_ref),
                (cell_hbm, cell_ref), (level_hbm, level_ref), (live_hbm, live_ref), (value_hbm, value_ref),
                (variance_hbm, variance_ref),
            )
        )
    ]
    for copy in local:
        copy.start()
    barrier = pltpu.get_barrier_semaphore()

    def greet(where):
        pl.semaphore_signal(barrier, inc=1, device_id=where, device_id_type=MESH)

    cross_north = jnp.logical_and(has_north, z_at == z_ring - 1)
    cross_south = jnp.logical_and(has_south, z_at == 0)

    @pl.when(cross_north)
    def _():
        greet({"grid": grid + 1})

    @pl.when(cross_south)
    def _():
        greet({"grid": grid - 1})

    for d in sorted(range(1, z_ring), key=lambda d: min(d, z_ring - d)):
        greet({"grid": z_peer(d)})
    for d in range(1, y_ring):
        greet({"grid": y_peer(d)})
    for d in range(1, n_mem):
        greet({"mem": mem_peer(d)})
    greeted = z_ring + y_ring + n_mem - 3 + cross_north.astype(jnp.int32) + cross_south.astype(jnp.int32)
    pl.semaphore_wait(barrier, greeted)

    def remote(src, dst, send, recv, where):
        return pltpu.make_async_remote_copy(
            src_ref=src, dst_ref=dst, send_sem=send, recv_sem=recv, device_id=where, device_id_type=MESH
        )

    north, south = {"grid": grid + 1}, {"grid": grid - 1}

    def halo(step, chunk):
        if step == 0:
            rows = pl.ds(8 * chunk, 8)
            src, below, above = first_hbm.at[rows], raw_south.at[rows], raw_north.at[rows]
        else:
            at = (step - 1, chunk)
            src, below, above = leaving.at[at], from_south.at[at], from_north.at[at]
        up = remote(src, below, s_halo.at[0, step, chunk], r_halo.at[0, step, chunk], north)
        down = remote(src, above, s_halo.at[1, step, chunk], r_halo.at[1, step, chunk], south)
        return up, down

    statics = (currents_hbm.at[1], kappa_hbm, mask_hbm)
    static_up = [
        remote(src, dst, s_static.at[0, index], r_static.at[0, index], north)
        for index, (src, dst) in enumerate(zip(statics, (v_south, k_south, mask_south)))
    ]
    static_down = [
        remote(src, dst, s_static.at[1, index], r_static.at[1, index], south)
        for index, (src, dst) in enumerate(zip(statics, (v_north, k_north, mask_north)))
    ]

    def start_halo(step, chunk):
        up, down = halo(step, chunk)
        pl.when(has_north)(up.start)
        pl.when(has_south)(down.start)

    for copy in static_up:
        pl.when(has_north)(copy.start)
    for copy in static_down:
        pl.when(has_south)(copy.start)
    for chunk in range(chunks):
        start_halo(0, chunk)

    @pl.when(jnp.logical_not(has_south))
    def _():
        v_south[...] = jnp.zeros_like(v_south)
        k_south[...] = jnp.zeros_like(k_south)
        mask_south[...] = jnp.zeros_like(mask_south)
        raw_south[...] = jnp.zeros_like(raw_south)
        from_south[...] = jnp.zeros_like(from_south)

    @pl.when(jnp.logical_not(has_north))
    def _():
        v_north[...] = jnp.zeros_like(v_north)
        k_north[...] = jnp.zeros_like(k_north)
        mask_north[...] = jnp.zeros_like(mask_north)
        raw_north[...] = jnp.zeros_like(raw_north)
        from_north[...] = jnp.zeros_like(from_north)

    def first_rows(ref, chunk, level):
        return ring(ref[8 * chunk : 8 * chunk + 8, level, 0, :], wide)

    for copy in local:
        copy.wait()
    for chunk in range(chunks):
        for level in range(levels):
            states[0, chunk, level] = first_rows(first_ref, chunk, level)
    slots = cell_ref.shape[0]
    place = (level_ref[...] * wide + cell_ref[...]).reshape(1, slots) - mem * unit_wide
    inside = jnp.logical_and(place >= 0, place < unit_wide)
    live = lax.broadcasted_iota(jnp.int32, (1, slots), 1) < live_ref[0]
    weight = jnp.where(jnp.logical_and(inside, live), 1.0 / jnp.sqrt(variance_ref[...].reshape(1, slots)), 0.0)
    picks[...] = jnp.where(
        lax.broadcasted_iota(jnp.int32, (unit_wide, slots), 0) == place, 1.0, 0.0
    ).astype(jnp.bfloat16)

    def rows_of(ref):
        return ring(ref[:, 0, :], wide)

    def sea_of(ref):
        return jnp.broadcast_to(ring(ref[...].astype(jnp.float32), wide), (levels, wide))

    zonal, velocity = ring(currents_ref[0, :, 0, :], wide), ring(currents_ref[1, :, 0, :], wide)
    kappa, sea = rows_of(kappa_ref), sea_of(mask_ref)
    a_east, b_east = faces(
        zonal, pltpu.roll(zonal, wide - 1, 1), kappa, pltpu.roll(kappa, wide - 1, 1), sea, pltpu.roll(sea, wide - 1, 1)
    )
    a_west, b_west = pltpu.roll(a_east, 1, 1), pltpu.roll(b_east, 1, 1)

    for copy in static_up:
        pl.when(has_south)(copy.wait_recv)
    for copy in static_down:
        pl.when(has_north)(copy.wait_recv)
    a_north, b_north = faces(velocity, rows_of(v_north), kappa, rows_of(k_north), sea, sea_of(mask_north))
    a_south, b_south = faces(rows_of(v_south), velocity, rows_of(k_south), kappa, sea_of(mask_south), sea)
    depth = lax.broadcasted_iota(jnp.int32, (levels, wide), 0)
    vertical = VERTICAL_MIX * sea
    borders = jnp.where(jnp.logical_or(depth == 0, depth == levels - 1), 1.0, 2.0)
    relax = jnp.where(depth == 0, 1.0 - SURFACE_RELAX * sea, 1.0)
    centre = 1.0 - a_east + b_west - a_north + b_south - borders * vertical
    parts = (centre, -b_east, a_west, -b_north, a_south, vertical, AGE_RATE * sea)
    for index, values in enumerate(parts):
        values = values * relax
        for level in range(levels):
            coefs[level, index] = jnp.broadcast_to(values[level : level + 1], (8, wide))

    full = wide - LANES
    last_lanes = lon - full
    tail_lane = lax.broadcasted_iota(jnp.int32, (8, LANES), 1)
    for step in range(STEPS):
        for chunk in range(chunks):
            up, down = halo(step, chunk)
            pl.when(has_south)(up.wait_recv)
            pl.when(has_north)(down.wait_recv)
            for level in range(levels):
                def at(which):
                    return states[step, chunk, which]

                if step == 0:
                    above, below = first_rows(raw_north, chunk, level), first_rows(raw_south, chunk, level)
                else:
                    above = spread_row(from_north.at[step - 1, chunk], level, levels, lon, wide)
                    below = spread_row(from_south.at[step - 1, chunk], level, levels, lon, wide)
                here = at(level)
                around = at(level - 1) if level > 0 else 0.0
                if level < levels - 1:
                    around = around + at(level + 1)
                result = (
                    coefs[level, 0] * here
                    + coefs[level, 1] * pltpu.roll(here, wide - 1, 1)
                    + coefs[level, 2] * pltpu.roll(here, 1, 1)
                    + coefs[level, 3] * above
                    + coefs[level, 4] * below
                    + coefs[level, 5] * around
                    + coefs[level, 6]
                )
                if step < STEPS - 1:
                    states[step + 1, chunk, level] = result
                    leaving[step, chunk, :, level * full : (level + 1) * full] = result[:, :full]
                    moved = result[:, full:] if level == 0 else pltpu.roll(result[:, full:], level * last_lanes, 1)
                    packed = moved if level == 0 else jnp.where(tail_lane < level * last_lanes, packed, moved)
                else:
                    for half in range(halves):
                        units[level * halves + half, chunk] = result[:, half * unit_wide : (half + 1) * unit_wide]
            if step < STEPS - 1:
                leaving[step, chunk, :, levels * full :] = packed
                start_halo(step + 1, chunk)
            else:
                rows = pl.ds(pl.multiple_of(mem * own + 8 * chunk, 8), 8)
                for d in range(1, n_mem):
                    remote(
                        units.at[mem_peer(d), chunk], own_all.at[rows], s_out.at[d - 1, chunk], r_out.at[d - 1, chunk],
                        {"mem": mem_peer(d)},
                    ).start()
                own_all[rows, :] = units[mem, chunk]

    def exchange(src_of, dst_of, send, recv, peers, axis, peer):
        return [remote(src_of(d), dst_of(d), send.at[d - 1], recv.at[d - 1], {axis: peer(d)}) for d in range(1, peers)]

    outs = [
        remote(
            units.at[mem_peer(d), chunk],
            own_all.at[pl.ds(pl.multiple_of(mem * own + 8 * chunk, 8), 8)],
            s_out.at[d - 1, chunk], r_out.at[d - 1, chunk], {"mem": mem_peer(d)},
        )
        for d in range(1, n_mem)
        for chunk in range(chunks)
    ]
    for copy in outs:
        copy.wait_recv()

    fields = own_all[...]
    high = fields.astype(jnp.bfloat16)
    rest = fields - high.astype(jnp.float32)
    middle = rest.astype(jnp.bfloat16)
    low = (rest - middle.astype(jnp.float32)).astype(jnp.bfloat16)
    seen = (
        jnp.dot(high, picks[...], preferred_element_type=jnp.float32)
        + jnp.dot(middle, picks[...], preferred_element_type=jnp.float32)
        + jnp.dot(low, picks[...], preferred_element_type=jnp.float32)
    )
    root = math.sqrt(count)
    inner = 1.0 / (count * (1.0 / root + 1.0))
    last = lax.broadcasted_iota(jnp.int32, (count, slots), 0) == count - 1
    everyone = jnp.sum(seen, axis=0, keepdims=True)
    final = seen[count - 1 : count]
    shared = -inner * (everyone - final) - final / root
    stacked = jnp.where(last, value_ref[...].reshape(1, slots) - everyone / count, seen + shared) * weight
    part[...] = lax.dot_general(
        stacked, stacked, (((1,), (1,)), ((), ())), precision=HIGHEST, preferred_element_type=jnp.float32
    ).reshape(n_mem, own, count)

    slices = exchange(lambda d: part.at[mem_peer(d)], lambda d: slice_parts.at[d - 1], s_slice, r_slice, n_mem, "mem", mem_peer)
    for copy in slices:
        copy.start()
    for copy in slices:
        copy.wait_recv()
    z_own[...] = part[mem] + jnp.sum(slice_parts[...], axis=0)
    along_z = exchange(lambda d: z_own, lambda d: z_parts.at[d - 1], s_z, r_z, z_ring, "grid", z_peer)
    for copy in along_z:
        copy.start()
    for copy in along_z:
        copy.wait_recv()
    y_own[...] = z_own[...] + jnp.sum(z_parts[...], axis=0)
    along_y = exchange(lambda d: y_own, lambda d: y_parts.at[d - 1], s_y, r_y, y_ring, "grid", y_peer)
    for copy in along_y:
        copy.start()
    for copy in along_y:
        copy.wait_recv()
    total[...] = y_own[...] + jnp.sum(y_parts[...], axis=0)
    gathered = exchange(lambda d: total, lambda d: gram.at[mem], s_all, r_all, n_mem, "mem", mem_peer)
    for copy in gathered:
        copy.start()
    gram[mem] = total[...]
    for copy in gathered:
        copy.wait_recv()

    inverse = factor_inverse(gram[...].reshape(count, count), count)
    square_lane = lax.broadcasted_iota(jnp.int32, (count, count), 1)
    square_row = lax.broadcasted_iota(jnp.int32, (count, count), 0)
    leading = jnp.where(square_lane < count - 1, inverse, 0.0)
    across = jnp.sum(leading, axis=1, keepdims=True)
    turned = jnp.where(square_lane == count - 1, -across / root, leading - inner * across)
    shift = -turned[count - 1 : count] / inverse[count - 1 : count, count - 1 : count]
    kept = jnp.where(square_row < count - 1, turned, 0.0)
    down_sum = jnp.sum(kept, axis=0, keepdims=True)
    spread = jnp.where(square_row == count - 1, -down_sum / root, kept - inner * down_sum)
    mixing = 1.0 / count + shift + math.sqrt(count - 1) * spread
    mixed[...] = jnp.dot(mixing, own_all[...], precision=HIGHEST).reshape(n_mem, own, unit_wide)
    mine = (
        mem // halves,
        slice(None),
        pl.ds(pl.multiple_of(lax.rem(mem, halves) * unit_wide, LANES), unit_wide),
    )
    back = exchange(lambda d: mixed.at[mem_peer(d)], lambda d: landed.at[mine], s_back, r_back, n_mem, "mem", mem_peer)
    for copy in back:
        copy.start()
    landed[mine] = mixed[mem]
    for copy in back:
        copy.wait_recv()
    for level in range(levels):
        out_ref[level] = landed[level][:, : out_ref.shape[2]]

    for step in range(STEPS):
        for chunk in range(chunks):
            up, down = halo(step, chunk)
            pl.when(has_north)(up.wait_send)
            pl.when(has_south)(down.wait_send)
    for copy in static_up:
        pl.when(has_north)(copy.wait_send)
    for copy in static_down:
        pl.when(has_south)(copy.wait_send)
    for copy in outs + slices + along_z + along_y + gathered + back:
        copy.wait_send()


def per_device(
    n_grid, n_mem, z_ring,
    background_elapsed_years, currents, diffusivity, sea_mask, observed_cell, measured_layer_number, live_counts,
    observed_value, error_variance,
):
    own, levels, _, lon = background_elapsed_years.shape
    chunks, slots = own // 8, observed_cell.shape[0]
    halves = n_mem // levels
    block = LANES * halves
    wide = -(-(lon + 2 * STEPS) // block) * block
    unit_wide = wide // halves
    y_ring = n_grid // z_ring
    count = own * n_mem
    f32 = jnp.float32
    dma = pltpu.SemaphoreType.DMA
    packed_shape = (STEPS - 1, chunks, 8, levels * (wide - LANES) + LANES)
    halo_shape = (STEPS, chunks, levels, 8, wide)
    i32 = jnp.int32
    scratch = [
        pltpu.VMEM((own, levels, 1, lon), f32),
        pltpu.VMEM((2, levels, 1, lon), f32),
        pltpu.VMEM((levels, 1, lon), f32),
        pltpu.VMEM((1, lon), i32),
        pltpu.VMEM((slots,), i32),
        pltpu.VMEM((slots,), i32),
        pltpu.SMEM((1,), i32),
        pltpu.VMEM((slots,), f32),
        pltpu.VMEM((slots,), f32),
        pltpu.VMEM(halo_shape, f32),
        pltpu.VMEM(packed_shape, f32),
        pltpu.VMEM((own, levels, 1, lon), f32),
        pltpu.VMEM((own, levels, 1, lon), f32),
        pltpu.VMEM(packed_shape, f32),
        pltpu.VMEM(packed_shape, f32),
        pltpu.VMEM((levels, 1, lon), f32),
        pltpu.VMEM((levels, 1, lon), f32),
        pltpu.VMEM((levels, 1, lon), f32),
        pltpu.VMEM((levels, 1, lon), f32),
        pltpu.VMEM((1, lon), i32),
        pltpu.VMEM((1, lon), i32),
        pltpu.VMEM((levels, 7, 8, wide), f32),
        pltpu.VMEM((n_mem, chunks, 8, unit_wide), f32),
        pltpu.VMEM((count, unit_wide), f32),
        pltpu.VMEM((unit_wide, slots), jnp.bfloat16),
        pltpu.VMEM((n_mem, own, count), f32),
        pltpu.VMEM((n_mem - 1, own, count), f32),
        pltpu.VMEM((own, count), f32),
        pltpu.VMEM((y_ring - 1, own, count), f32),
        pltpu.VMEM((own, count), f32),
        pltpu.VMEM((z_ring - 1, own, count), f32),
        pltpu.VMEM((own, count), f32),
        pltpu.VMEM((n_mem, own, count), f32),
        pltpu.VMEM((n_mem, own, unit_wide), f32),
        pltpu.VMEM((levels, own, wide), f32),
    ]
    semaphores = [
        dma((9,)),
        dma((2, STEPS, chunks)), dma((2, STEPS, chunks)),
        dma((2, 3)), dma((2, 3)),
        dma((n_mem - 1, chunks)), dma((n_mem - 1, chunks)),
        dma((n_mem - 1,)), dma((n_mem - 1,)),
        dma((z_ring - 1,)), dma((z_ring - 1,)),
        dma((y_ring - 1,)), dma((y_ring - 1,)),
        dma((n_mem - 1,)), dma((n_mem - 1,)),
        dma((n_mem - 1,)), dma((n_mem - 1,)),
    ]
    result = pl.pallas_call(
        functools.partial(kernel, (n_grid, n_mem, z_ring, levels, lon, wide, chunks)),
        out_shape=pltpu.VMEM((levels, own, lon), f32),
        in_specs=[pl.BlockSpec(memory_space=pltpu.HBM)] * 9,
        out_specs=pl.BlockSpec(memory_space=pltpu.VMEM),
        scratch_shapes=scratch + semaphores,
        compiler_params=pltpu.CompilerParams(
            collective_id=0, has_side_effects=True, vmem_limit_bytes=60 * 1024 * 1024
        ),
    )(
        background_elapsed_years, currents, diffusivity, sea_mask, observed_cell, measured_layer_number, live_counts,
        observed_value, error_variance,
    )
    return result.transpose(1, 0, 2)[:, :, None, :]


def solution(mesh):
    placed = (
        P("mem", None, "grid", None),
        P(None, None, "grid", None),
        P(None, "grid", None),
        P("grid", None),
        P("grid"),
        P("grid"),
        P("grid"),
        P("grid"),
        P("grid"),
    )
    return jax.shard_map(
        functools.partial(per_device, mesh.shape["grid"], mesh.shape["mem"], Z_RING),
        mesh=mesh,
        in_specs=placed,
        out_specs=P("mem", None, "grid", None),
        check_vma=False,
    )
```

```python
import functools
import math

import jax
import jax.numpy as jnp
from jax import lax
from jax.experimental import pallas as pl
from jax.experimental.pallas import tpu as pltpu
from jax.sharding import PartitionSpec as P

STEPS = 4
Z_RING = 12
LANES = 128
PANEL = 64
VERTICAL_MIX = 0.05
AGE_RATE = 0.25
SURFACE_RELAX = 0.5
HIGHEST = lax.Precision.HIGHEST
MESH = pl.DeviceIdType.MESH


def faces(speed_a, speed_b, kappa_a, kappa_b, sea_a, sea_b):
    speed = 0.5 * (speed_a + speed_b)
    kappa = 0.5 * (kappa_a + kappa_b)
    both = sea_a * sea_b
    return both * (jnp.maximum(speed, 0.0) + kappa), both * (jnp.minimum(speed, 0.0) - kappa)


def factor_inverse(gram, count):
    panel = min(PANEL, count)
    wide_row = lax.broadcasted_iota(jnp.int32, (panel, count), 0)
    lane = lax.broadcasted_iota(jnp.int32, (panel, count), 1)
    row = lax.broadcasted_iota(jnp.int32, (8, count), 0)
    full_row = lax.broadcasted_iota(jnp.int32, (count, count), 0)
    full_lane = lax.broadcasted_iota(jnp.int32, (count, count), 1)
    left = gram + jnp.where(full_row == full_lane, float(count - 1), 0.0)
    right = jnp.where(full_row == full_lane, 1.0, 0.0)
    done = []
    for first in range(0, count, panel):
        a_rest, e_rest = left[:panel], right[:panel]
        a_done, e_done = [], []
        for base in range(first, first + panel, 8):
            a, e, a_rest, e_rest = a_rest[:8], e_rest[:8], a_rest[8:], e_rest[8:]
            columns = [jnp.broadcast_to(a[:, base + j : base + j + 1], (8, count)) for j in range(8)]
            scales = []
            for k in range(0, 8, 2):
                now, later = columns[k], columns[k + 1]
                p, q, r = now[k : k + 1], now[k + 1 : k + 2], later[k + 1 : k + 2]
                per_pair, per_p = 1.0 / (p * r - q * q), 1.0 / p
                below_now, below_later = jnp.where(row > k + 1, now, 0.0), jnp.where(row > k + 1, later, 0.0)
                first_factor = (below_now * r - below_later * q) * per_pair
                later_factor = (below_later * p - below_now * q) * per_pair
                first_factor = jnp.where(row == k + 1, q * per_p, first_factor)
                for j in range(k + 2, 8):
                    at = columns[j]
                    columns[j] = at - (first_factor * at[k : k + 1] + later_factor * at[k + 1 : k + 2])
                a = a - (first_factor * a[k : k + 1] + later_factor * a[k + 1 : k + 2])
                e = e - (first_factor * e[k : k + 1] + later_factor * e[k + 1 : k + 2])
                scales += [per_p, per_pair * p]
            a_done.append(a)
            e_done.append(e)
            rows = first + panel - base - 8
            if rows:
                lower = [jnp.broadcast_to(a_rest[:, base + j : base + j + 1], (rows, count)) for j in range(8)]
                for k in range(8):
                    factor = lower[k] * scales[k]
                    for j in range(k + 1, 8):
                        lower[j] = lower[j] - factor * columns[j][k : k + 1]
                    a_rest = a_rest - factor * a[k : k + 1]
                    e_rest = e_rest - factor * e[k : k + 1]
        a, e = jnp.concatenate(a_done, 0), jnp.concatenate(e_done, 0)
        pivots = jnp.sum(jnp.where(lane == wide_row + first, a, 0.0), axis=1, keepdims=True)
        root = lax.rsqrt(pivots)
        a, e = a * root, e * root
        done.append(e)
        if first + panel < count:
            turned = jnp.transpose(a)[first + panel :]
            left = left[panel:] - jnp.dot(turned, a, precision=HIGHEST)
            right = right[panel:] - jnp.dot(turned, e, precision=HIGHEST)
    return jnp.concatenate(done, 0)


def fold_square(square, count):
    half = count // 2
    row = lax.broadcasted_iota(jnp.int32, (half, count), 0)
    lane = lax.broadcasted_iota(jnp.int32, (half, count), 1)
    upper, lower = pltpu.roll(square[:half], half, 1), square[half:]
    folded = jnp.where(jnp.logical_or(lane < half, row <= lane - half), upper, lower)
    return folded, jnp.sum(jnp.where(row == lane - half, lower, 0.0), axis=0, keepdims=True)


def unfold_square(folded, diagonal, count):
    half = count // 2
    row = lax.broadcasted_iota(jnp.int32, (count, count), 0)
    lane = lax.broadcasted_iota(jnp.int32, (count, count), 1)
    here = jnp.concatenate([pltpu.roll(folded, half, 1), folded], 0)
    turned = jnp.transpose(here)
    top = jnp.logical_and(row < half, row <= lane)
    bottom = jnp.logical_and(lane >= half, row > lane)
    square = jnp.where(jnp.logical_or(top, bottom), here, turned)
    return jnp.where(jnp.logical_and(row == lane, row >= half), diagonal, square)


def body_start(level, levels, full):
    return level * full + (LANES if level >= levels // 2 else 0)


def spread_row(flat, level, levels, lon, wide):
    full, last = wide - LANES, lon - (wide - LANES)
    start, shared = body_start(level, levels, full), levels // 2 * full
    body, packed = flat[:, start : start + full], flat[:, shared : shared + LANES]
    lane = lax.broadcasted_iota(jnp.int32, (8, LANES), 1)
    ending = packed if level == 0 else pltpu.roll(packed, LANES - level * last, 1)
    opening, closing = pltpu.roll(body[:, :LANES], last, 1), pltpu.roll(ending, LANES - last, 1)
    tail = jnp.where(lane < last + STEPS, jnp.where(lane < last, ending, opening), 0.0)
    return jnp.concatenate([body, jnp.where(lane >= LANES - STEPS, closing, tail)], 1)


def ring(x, wide):
    rows, lon = x.shape
    gap = jnp.zeros((rows, wide - lon - 2 * STEPS), x.dtype)
    return jnp.concatenate([x, x[:, :STEPS], gap, x[:, lon - STEPS :]], 1)


def kernel(
    cfg,
    first_hbm, currents_hbm, kappa_hbm, mask_hbm, cell_hbm, level_hbm, live_hbm, value_hbm, variance_hbm,
    out_ref,
    first_ref, currents_ref, kappa_ref, mask_ref, cell_ref, level_ref, live_ref, value_ref, variance_ref,
    states, leaving, raw_south, raw_north, from_south, from_north, v_south, v_north, k_south, k_north, mask_south, mask_north,
    coefs, units, own_all, picks, part, slice_parts, y_own, y_parts, z_own, z_parts, total, gram, mixed, landed,
    s_in, s_halo, r_halo, s_static, r_static, s_out, r_out, s_slice, r_slice, s_z, r_z, s_y, r_y,
    s_all, r_all, s_back, r_back,
):
    n_grid, n_mem, z_ring, levels, lon, wide, chunks = cfg
    y_ring = n_grid // z_ring
    own = 8 * chunks
    count = n_mem * own
    unit_wide = levels * wide // n_mem
    piece = unit_wide // 2
    pieces, pair = wide // piece, levels // 2
    full = wide - LANES
    grid = lax.axis_index("grid")
    mem = lax.axis_index("mem")
    y_at, z_at = grid // z_ring, lax.rem(grid, z_ring)
    has_north, has_south = grid < n_grid - 1, grid > 0

    def mem_peer(d):
        return lax.rem(mem + d, n_mem)

    def z_peer(d):
        return y_at * z_ring + lax.rem(z_at + d, z_ring)

    def y_peer(d):
        return lax.rem(y_at + d, y_ring) * z_ring + z_at

    local = [
        pltpu.make_async_copy(src, dst, s_in.at[index])
        for index, (src, dst) in enumerate(
            (
                (first_hbm, first_ref), (currents_hbm, currents_ref), (kappa_hbm, kappa_ref), (mask_hbm, mask_ref),
                (cell_hbm, cell_ref), (level_hbm, level_ref), (live_hbm, live_ref), (value_hbm, value_ref),
                (variance_hbm, variance_ref),
            )
        )
    ]
    for copy in local:
        copy.start()
    barrier = pltpu.get_barrier_semaphore()

    def greet(where):
        pl.semaphore_signal(barrier, inc=1, device_id=where, device_id_type=MESH)

    cross_north = jnp.logical_and(has_north, z_at == z_ring - 1)
    cross_south = jnp.logical_and(has_south, z_at == 0)

    @pl.when(cross_north)
    def _():
        greet({"grid": grid + 1})

    @pl.when(cross_south)
    def _():
        greet({"grid": grid - 1})

    for d in sorted(range(1, z_ring), key=lambda d: min(d, z_ring - d)):
        greet({"grid": z_peer(d)})
    for d in range(1, y_ring):
        greet({"grid": y_peer(d)})
    for d in range(1, n_mem):
        greet({"mem": mem_peer(d)})
    greeted = z_ring + y_ring + n_mem - 3 + cross_north.astype(jnp.int32) + cross_south.astype(jnp.int32)
    pl.semaphore_wait(barrier, greeted)

    def remote(src, dst, send, recv, where):
        return pltpu.make_async_remote_copy(
            src_ref=src, dst_ref=dst, send_sem=send, recv_sem=recv, device_id=where, device_id_type=MESH
        )

    north, south = {"grid": grid + 1}, {"grid": grid - 1}

    def halo(step, chunk):
        if step == 0:
            rows = pl.ds(8 * chunk, 8)
            src, below, above = first_hbm.at[rows], raw_south.at[rows], raw_north.at[rows]
        else:
            at = (step - 1, chunk)
            src, below, above = leaving.at[at], from_south.at[at], from_north.at[at]
        if step < STEPS - 1:
            trips = [(step, src, below, above)]
        else:
            early = pl.ds(0, pair * full + LANES)
            late = pl.ds(pair * full + LANES, (levels - pair) * full)
            trips = [
                (step + index, src.at[:, lanes], below.at[:, lanes], above.at[:, lanes])
                for index, lanes in enumerate((early, late))
            ]
        return [
            (
                remote(src, below, s_halo.at[0, at, chunk], r_halo.at[0, at, chunk], north),
                remote(src, above, s_halo.at[1, at, chunk], r_halo.at[1, at, chunk], south),
            )
            for at, src, below, above in trips
        ]

    statics = (currents_hbm.at[1], kappa_hbm, mask_hbm)
    static_up = [
        remote(src, dst, s_static.at[0, index], r_static.at[0, index], north)
        for index, (src, dst) in enumerate(zip(statics, (v_south, k_south, mask_south)))
    ]
    static_down = [
        remote(src, dst, s_static.at[1, index], r_static.at[1, index], south)
        for index, (src, dst) in enumerate(zip(statics, (v_north, k_north, mask_north)))
    ]

    def start_halo(step, chunk):
        for up, down in halo(step, chunk):
            pl.when(has_north)(up.start)
            pl.when(has_south)(down.start)

    for copy in static_up:
        pl.when(has_north)(copy.start)
    for copy in static_down:
        pl.when(has_south)(copy.start)
    for chunk in range(chunks):
        start_halo(0, chunk)

    @pl.when(jnp.logical_not(has_south))
    def _():
        v_south[...] = jnp.zeros_like(v_south)
        k_south[...] = jnp.zeros_like(k_south)
        mask_south[...] = jnp.zeros_like(mask_south)
        raw_south[...] = jnp.zeros_like(raw_south)
        from_south[...] = jnp.zeros_like(from_south)

    @pl.when(jnp.logical_not(has_north))
    def _():
        v_north[...] = jnp.zeros_like(v_north)
        k_north[...] = jnp.zeros_like(k_north)
        mask_north[...] = jnp.zeros_like(mask_north)
        raw_north[...] = jnp.zeros_like(raw_north)
        from_north[...] = jnp.zeros_like(from_north)

    def first_rows(ref, chunk, level):
        return ring(ref[8 * chunk : 8 * chunk + 8, level, 0, :], wide)

    for copy in local:
        copy.wait()
    for chunk in range(chunks):
        for level in range(levels):
            states[0, chunk, level] = first_rows(first_ref, chunk, level)
    slots = cell_ref.shape[0]
    upper_pair = jnp.where(level_ref[...] >= pair, 1, 0)
    flat = (level_ref[...] - upper_pair * pair) * wide + cell_ref[...] - mem * piece
    place = jnp.where(jnp.logical_and(flat >= 0, flat < piece), flat + upper_pair * piece, -1).reshape(1, slots)
    inside = place >= 0
    live = lax.broadcasted_iota(jnp.int32, (1, slots), 1) < live_ref[0]
    weight = jnp.where(jnp.logical_and(inside, live), 1.0 / jnp.sqrt(variance_ref[...].reshape(1, slots)), 0.0)
    picks[...] = jnp.where(
        lax.broadcasted_iota(jnp.int32, (unit_wide, slots), 0) == place, 1.0, 0.0
    ).astype(jnp.bfloat16)

    def rows_of(ref):
        return ring(ref[:, 0, :], wide)

    def sea_of(ref):
        return jnp.broadcast_to(ring(ref[...].astype(jnp.float32), wide), (levels, wide))

    zonal, velocity = ring(currents_ref[0, :, 0, :], wide), ring(currents_ref[1, :, 0, :], wide)
    kappa, sea = rows_of(kappa_ref), sea_of(mask_ref)
    a_east, b_east = faces(
        zonal, pltpu.roll(zonal, wide - 1, 1), kappa, pltpu.roll(kappa, wide - 1, 1), sea, pltpu.roll(sea, wide - 1, 1)
    )
    a_west, b_west = pltpu.roll(a_east, 1, 1), pltpu.roll(b_east, 1, 1)

    for copy in static_up:
        pl.when(has_south)(copy.wait_recv)
    for copy in static_down:
        pl.when(has_north)(copy.wait_recv)
    a_north, b_north = faces(velocity, rows_of(v_north), kappa, rows_of(k_north), sea, sea_of(mask_north))
    a_south, b_south = faces(rows_of(v_south), velocity, rows_of(k_south), kappa, sea_of(mask_south), sea)
    depth = lax.broadcasted_iota(jnp.int32, (levels, wide), 0)
    vertical = VERTICAL_MIX * sea
    borders = jnp.where(jnp.logical_or(depth == 0, depth == levels - 1), 1.0, 2.0)
    relax = jnp.where(depth == 0, 1.0 - SURFACE_RELAX * sea, 1.0)
    centre = 1.0 - a_east + b_west - a_north + b_south - borders * vertical
    parts = (centre, -b_east, a_west, -b_north, a_south, vertical, AGE_RATE * sea)
    for index, values in enumerate(parts):
        values = values * relax
        for level in range(levels):
            coefs[level, index] = jnp.broadcast_to(values[level : level + 1], (8, wide))

    def landing(chunk, which):
        return pl.ds(pl.multiple_of(mem * own + 8 * chunk, 8), 8), pl.ds(which * piece, piece)

    def sent(chunk, which):
        return [
            remote(
                units.at[mem_peer(d), chunk, which], own_all.at[landing(chunk, which)],
                s_out.at[d - 1, chunk, which], r_out.at[d - 1, chunk, which], {"mem": mem_peer(d)},
            )
            for d in range(1, n_mem)
        ]

    last_lanes = lon - full
    tail_lane = lax.broadcasted_iota(jnp.int32, (8, LANES), 1)
    for step in range(STEPS):
        for chunk in range(chunks):
            arriving = halo(step, chunk)
            for level in range(levels):
                if level % (levels // len(arriving)) == 0:
                    up, down = arriving[level * len(arriving) // levels]
                    pl.when(has_south)(up.wait_recv)
                    pl.when(has_north)(down.wait_recv)

                def at(which):
                    return states[step, chunk, which]

                if step == 0:
                    above, below = first_rows(raw_north, chunk, level), first_rows(raw_south, chunk, level)
                else:
                    above = spread_row(from_north.at[step - 1, chunk], level, levels, lon, wide)
                    below = spread_row(from_south.at[step - 1, chunk], level, levels, lon, wide)
                here = at(level)
                around = at(level - 1) if level > 0 else 0.0
                if level < levels - 1:
                    around = around + at(level + 1)
                result = (
                    coefs[level, 0] * here
                    + coefs[level, 1] * pltpu.roll(here, wide - 1, 1)
                    + coefs[level, 2] * pltpu.roll(here, 1, 1)
                    + coefs[level, 3] * above
                    + coefs[level, 4] * below
                    + coefs[level, 5] * around
                    + coefs[level, 6]
                )
                if step < STEPS - 1:
                    states[step + 1, chunk, level] = result
                    start = body_start(level, levels, full)
                    leaving[step, chunk, :, start : start + full] = result[:, :full]
                    moved = result[:, full:] if level == 0 else pltpu.roll(result[:, full:], level * last_lanes, 1)
                    packed = moved if level == 0 else jnp.where(tail_lane < level * last_lanes, packed, moved)
                else:
                    for index in range(pieces):
                        units[level % pair * pieces + index, chunk, level // pair] = result[
                            :, index * piece : (index + 1) * piece
                        ]
                    if level % pair == pair - 1:
                        for copy in sent(chunk, level // pair):
                            copy.start()
                        rows, lanes = landing(chunk, level // pair)
                        own_all[rows, lanes] = units[mem, chunk, level // pair]
            if step < STEPS - 1:
                leaving[step, chunk, :, pair * full : pair * full + LANES] = packed
                start_halo(step + 1, chunk)

    def exchange(src_of, dst_of, send, recv, peers, axis, peer):
        return [remote(src_of(d), dst_of(d), send.at[d - 1], recv.at[d - 1], {axis: peer(d)}) for d in range(1, peers)]

    outs = [copy for chunk in range(chunks) for which in range(2) for copy in sent(chunk, which)]
    for copy in outs:
        copy.wait_recv()

    fields = own_all[...]
    high = fields.astype(jnp.bfloat16)
    rest = fields - high.astype(jnp.float32)
    middle = rest.astype(jnp.bfloat16)
    low = (rest - middle.astype(jnp.float32)).astype(jnp.bfloat16)
    seen = (
        jnp.dot(high, picks[...], preferred_element_type=jnp.float32)
        + jnp.dot(middle, picks[...], preferred_element_type=jnp.float32)
        + jnp.dot(low, picks[...], preferred_element_type=jnp.float32)
    )
    root = math.sqrt(count)
    inner = 1.0 / (count * (1.0 / root + 1.0))
    last = lax.broadcasted_iota(jnp.int32, (count, slots), 0) == count - 1
    everyone = jnp.sum(seen, axis=0, keepdims=True)
    final = seen[count - 1 : count]
    shared = -inner * (everyone - final) - final / root
    stacked = jnp.where(last, value_ref[...].reshape(1, slots) - everyone / count, seen + shared) * weight
    folded, diagonal = fold_square(lax.dot_general(
        stacked, stacked, (((1,), (1,)), ((), ())), precision=HIGHEST, preferred_element_type=jnp.float32
    ), count)
    share = count // 2 // n_mem
    for index in range(n_mem):
        part[index, :share] = folded[index * share : (index + 1) * share]
        part[index, share:] = diagonal

    slices = exchange(lambda d: part.at[mem_peer(d)], lambda d: slice_parts.at[d - 1], s_slice, r_slice, n_mem, "mem", mem_peer)
    for copy in slices:
        copy.start()
    for copy in slices:
        copy.wait_recv()
    z_own[...] = part[mem] + jnp.sum(slice_parts[...], axis=0)
    along_z = exchange(lambda d: z_own, lambda d: z_parts.at[d - 1], s_z, r_z, z_ring, "grid", z_peer)
    for copy in along_z:
        copy.start()
    for copy in along_z:
        copy.wait_recv()
    y_own[...] = z_own[...] + jnp.sum(z_parts[...], axis=0)
    along_y = exchange(lambda d: y_own, lambda d: y_parts.at[d - 1], s_y, r_y, y_ring, "grid", y_peer)
    for copy in along_y:
        copy.start()
    for copy in along_y:
        copy.wait_recv()
    total[...] = y_own[...] + jnp.sum(y_parts[...], axis=0)
    gathered = exchange(lambda d: total, lambda d: gram.at[mem], s_all, r_all, n_mem, "mem", mem_peer)
    for copy in gathered:
        copy.start()
    gram[mem] = total[...]
    for copy in gathered:
        copy.wait_recv()

    folded = jnp.concatenate([gram[index, :share] for index in range(n_mem)], 0)
    inverse = factor_inverse(unfold_square(folded, gram[0, share:], count), count)
    square_lane = lax.broadcasted_iota(jnp.int32, (count, count), 1)
    square_row = lax.broadcasted_iota(jnp.int32, (count, count), 0)
    leading = jnp.where(square_lane < count - 1, inverse, 0.0)
    across = jnp.sum(leading, axis=1, keepdims=True)
    turned = jnp.where(square_lane == count - 1, -across / root, leading - inner * across)
    shift = -turned[count - 1 : count] / inverse[count - 1 : count, count - 1 : count]
    kept = jnp.where(square_row < count - 1, turned, 0.0)
    down_sum = jnp.sum(kept, axis=0, keepdims=True)
    spread = jnp.where(square_row == count - 1, -down_sum / root, kept - inner * down_sum)
    mixing = 1.0 / count + shift + math.sqrt(count - 1) * spread
    mixed[...] = jnp.dot(mixing, own_all[...], precision=HIGHEST).reshape(n_mem, own, unit_wide)
    back = exchange(lambda d: mixed.at[mem_peer(d)], lambda d: landed.at[mem], s_back, r_back, n_mem, "mem", mem_peer)
    for copy in back:
        copy.start()
    landed[mem] = mixed[mem]
    for copy in back:
        copy.wait_recv()
    for member in range(n_mem):
        for which in range(2):
            lane = member % pieces * piece
            count_here = min(piece, lon - lane)
            out_ref[which * pair + member // pieces, :, lane : lane + count_here] = landed[
                member, :, which * piece : which * piece + count_here
            ]

    for step in range(STEPS):
        for chunk in range(chunks):
            for up, down in halo(step, chunk):
                pl.when(has_north)(up.wait_send)
                pl.when(has_south)(down.wait_send)
    for copy in static_up:
        pl.when(has_north)(copy.wait_send)
    for copy in static_down:
        pl.when(has_south)(copy.wait_send)
    for copy in outs + slices + along_z + along_y + gathered + back:
        copy.wait_send()


def per_device(
    n_grid, n_mem, z_ring,
    background_elapsed_years, currents, diffusivity, sea_mask, observed_cell, measured_layer_number, live_counts,
    observed_value, error_variance,
):
    own, levels, _, lon = background_elapsed_years.shape
    chunks, slots = own // 8, observed_cell.shape[0]
    halves = n_mem // levels
    block = LANES * halves
    wide = -(-(lon + 2 * STEPS) // block) * block
    unit_wide = levels * wide // n_mem
    y_ring = n_grid // z_ring
    count = own * n_mem
    f32 = jnp.float32
    dma = pltpu.SemaphoreType.DMA
    packed_shape = (STEPS - 1, chunks, 8, levels * (wide - LANES) + LANES)
    halo_shape = (STEPS, chunks, levels, 8, wide)
    i32 = jnp.int32
    scratch = [
        pltpu.VMEM((own, levels, 1, lon), f32),
        pltpu.VMEM((2, levels, 1, lon), f32),
        pltpu.VMEM((levels, 1, lon), f32),
        pltpu.VMEM((1, lon), i32),
        pltpu.VMEM((slots,), i32),
        pltpu.VMEM((slots,), i32),
        pltpu.SMEM((1,), i32),
        pltpu.VMEM((slots,), f32),
        pltpu.VMEM((slots,), f32),
        pltpu.VMEM(halo_shape, f32),
        pltpu.VMEM(packed_shape, f32),
        pltpu.VMEM((own, levels, 1, lon), f32),
        pltpu.VMEM((own, levels, 1, lon), f32),
        pltpu.VMEM(packed_shape, f32),
        pltpu.VMEM(packed_shape, f32),
        pltpu.VMEM((levels, 1, lon), f32),
        pltpu.VMEM((levels, 1, lon), f32),
        pltpu.VMEM((levels, 1, lon), f32),
        pltpu.VMEM((levels, 1, lon), f32),
        pltpu.VMEM((1, lon), i32),
        pltpu.VMEM((1, lon), i32),
        pltpu.VMEM((levels, 7, 8, wide), f32),
        pltpu.VMEM((n_mem, chunks, 2, 8, unit_wide // 2), f32),
        pltpu.VMEM((count, unit_wide), f32),
        pltpu.VMEM((unit_wide, slots), jnp.bfloat16),
        pltpu.VMEM((n_mem, count // 2 // n_mem + 1, count), f32),
        pltpu.VMEM((n_mem - 1, count // 2 // n_mem + 1, count), f32),
        pltpu.VMEM((count // 2 // n_mem + 1, count), f32),
        pltpu.VMEM((y_ring - 1, count // 2 // n_mem + 1, count), f32),
        pltpu.VMEM((count // 2 // n_mem + 1, count), f32),
        pltpu.VMEM((z_ring - 1, count // 2 // n_mem + 1, count), f32),
        pltpu.VMEM((count // 2 // n_mem + 1, count), f32),
        pltpu.VMEM((n_mem, count // 2 // n_mem + 1, count), f32),
        pltpu.VMEM((n_mem, own, unit_wide), f32),
        pltpu.VMEM((n_mem, own, unit_wide), f32),
    ]
    semaphores = [
        dma((9,)),
        dma((2, STEPS + 1, chunks)), dma((2, STEPS + 1, chunks)),
        dma((2, 3)), dma((2, 3)),
        dma((n_mem - 1, chunks, 2)), dma((n_mem - 1, chunks, 2)),
        dma((n_mem - 1,)), dma((n_mem - 1,)),
        dma((z_ring - 1,)), dma((z_ring - 1,)),
        dma((y_ring - 1,)), dma((y_ring - 1,)),
        dma((n_mem - 1,)), dma((n_mem - 1,)),
        dma((n_mem - 1,)), dma((n_mem - 1,)),
    ]
    result = pl.pallas_call(
        functools.partial(kernel, (n_grid, n_mem, z_ring, levels, lon, wide, chunks)),
        out_shape=pltpu.VMEM((levels, own, lon), f32),
        in_specs=[pl.BlockSpec(memory_space=pltpu.HBM)] * 9,
        out_specs=pl.BlockSpec(memory_space=pltpu.VMEM),
        scratch_shapes=scratch + semaphores,
        compiler_params=pltpu.CompilerParams(
            collective_id=0, has_side_effects=True, vmem_limit_bytes=60 * 1024 * 1024
        ),
    )(
        background_elapsed_years, currents, diffusivity, sea_mask, observed_cell, measured_layer_number, live_counts,
        observed_value, error_variance,
    )
    return result.transpose(1, 0, 2)[:, :, None, :]


def solution(mesh):
    placed = (
        P("mem", None, "grid", None),
        P(None, None, "grid", None),
        P(None, "grid", None),
        P("grid", None),
        P("grid"),
        P("grid"),
        P("grid"),
        P("grid"),
        P("grid"),
    )
    return jax.shard_map(
        functools.partial(per_device, mesh.shape["grid"], mesh.shape["mem"], Z_RING),
        mesh=mesh,
        in_specs=placed,
        out_specs=P("mem", None, "grid", None),
        check_vma=False,
    )
```

```python
import functools
import math

import jax
import jax.numpy as jnp
from jax import lax
from jax.experimental import pallas as pl
from jax.experimental.pallas import tpu as pltpu
from jax.sharding import PartitionSpec as P

STEPS = 4
Z_RING = 12
LANES = 128
PANEL = 64
VERTICAL_MIX = 0.05
AGE_RATE = 0.25
SURFACE_RELAX = 0.5
HIGHEST = lax.Precision.HIGHEST
MESH = pl.DeviceIdType.MESH


def faces(speed_a, speed_b, kappa_a, kappa_b, sea_a, sea_b):
    speed = 0.5 * (speed_a + speed_b)
    kappa = 0.5 * (kappa_a + kappa_b)
    both = sea_a * sea_b
    return both * (jnp.maximum(speed, 0.0) + kappa), both * (jnp.minimum(speed, 0.0) - kappa)


def factor_inverse(gram, count):
    panel = min(PANEL, count)
    wide_row = lax.broadcasted_iota(jnp.int32, (panel, count), 0)
    lane = lax.broadcasted_iota(jnp.int32, (panel, count), 1)
    row = lax.broadcasted_iota(jnp.int32, (8, count), 0)
    full_row = lax.broadcasted_iota(jnp.int32, (count, count), 0)
    full_lane = lax.broadcasted_iota(jnp.int32, (count, count), 1)
    left = gram + jnp.where(full_row == full_lane, float(count - 1), 0.0)
    right = jnp.where(full_row == full_lane, 1.0, 0.0)
    done = []
    for first in range(0, count, panel):
        a_rest, e_rest = left[:panel], right[:panel]
        a_done, e_done = [], []
        for base in range(first, first + panel, 8):
            a, e, a_rest, e_rest = a_rest[:8], e_rest[:8], a_rest[8:], e_rest[8:]
            columns = [jnp.broadcast_to(a[:, base + j : base + j + 1], (8, count)) for j in range(8)]
            scales = []
            for k in range(0, 8, 2):
                now, later = columns[k], columns[k + 1]
                p, q, r = now[k : k + 1], now[k + 1 : k + 2], later[k + 1 : k + 2]
                per_pair, per_p = 1.0 / (p * r - q * q), 1.0 / p
                below_now, below_later = jnp.where(row > k + 1, now, 0.0), jnp.where(row > k + 1, later, 0.0)
                first_factor = (below_now * r - below_later * q) * per_pair
                later_factor = (below_later * p - below_now * q) * per_pair
                first_factor = jnp.where(row == k + 1, q * per_p, first_factor)
                for j in range(k + 2, 8):
                    at = columns[j]
                    columns[j] = at - (first_factor * at[k : k + 1] + later_factor * at[k + 1 : k + 2])
                a = a - (first_factor * a[k : k + 1] + later_factor * a[k + 1 : k + 2])
                e = e - (first_factor * e[k : k + 1] + later_factor * e[k + 1 : k + 2])
                scales += [per_p, per_pair * p]
            a_done.append(a)
            e_done.append(e)
            rows = first + panel - base - 8
            if rows:
                lower = [jnp.broadcast_to(a_rest[:, base + j : base + j + 1], (rows, count)) for j in range(8)]
                for k in range(8):
                    factor = lower[k] * scales[k]
                    for j in range(k + 1, 8):
                        lower[j] = lower[j] - factor * columns[j][k : k + 1]
                    a_rest = a_rest - factor * a[k : k + 1]
                    e_rest = e_rest - factor * e[k : k + 1]
        a, e = jnp.concatenate(a_done, 0), jnp.concatenate(e_done, 0)
        pivots = jnp.sum(jnp.where(lane == wide_row + first, a, 0.0), axis=1, keepdims=True)
        root = lax.rsqrt(pivots)
        a, e = a * root, e * root
        done.append(e)
        if first + panel < count:
            turned = jnp.transpose(a)[first + panel :]
            left = left[panel:] - jnp.dot(turned, a, precision=HIGHEST)
            right = right[panel:] - jnp.dot(turned, e, precision=HIGHEST)
    return jnp.concatenate(done, 0)


def fold_square(square, count):
    half = count // 2
    row = lax.broadcasted_iota(jnp.int32, (half, count), 0)
    lane = lax.broadcasted_iota(jnp.int32, (half, count), 1)
    upper, lower = pltpu.roll(square[:half], half, 1), square[half:]
    folded = jnp.where(jnp.logical_or(lane < half, row <= lane - half), upper, lower)
    return folded, jnp.sum(jnp.where(row == lane - half, lower, 0.0), axis=0, keepdims=True)


def unfold_square(folded, diagonal, count):
    half = count // 2
    row = lax.broadcasted_iota(jnp.int32, (count, count), 0)
    lane = lax.broadcasted_iota(jnp.int32, (count, count), 1)
    here = jnp.concatenate([pltpu.roll(folded, half, 1), folded], 0)
    turned = jnp.transpose(here)
    top = jnp.logical_and(row < half, row <= lane)
    bottom = jnp.logical_and(lane >= half, row > lane)
    square = jnp.where(jnp.logical_or(top, bottom), here, turned)
    return jnp.where(jnp.logical_and(row == lane, row >= half), diagonal, square)


def far_first(peers):
    return sorted(range(1, peers), key=lambda d: -min(d, peers - d))


def body_start(level, levels, full):
    return level * full + (LANES if level >= levels // 2 else 0)


def spread_row(flat, level, levels, lon, wide):
    full, last = wide - LANES, lon - (wide - LANES)
    start, shared = body_start(level, levels, full), levels // 2 * full
    body, packed = flat[:, start : start + full], flat[:, shared : shared + LANES]
    lane = lax.broadcasted_iota(jnp.int32, (8, LANES), 1)
    ending = packed if level == 0 else pltpu.roll(packed, LANES - level * last, 1)
    opening, closing = pltpu.roll(body[:, :LANES], last, 1), pltpu.roll(ending, LANES - last, 1)
    tail = jnp.where(lane < last + STEPS, jnp.where(lane < last, ending, opening), 0.0)
    return jnp.concatenate([body, jnp.where(lane >= LANES - STEPS, closing, tail)], 1)


def ring(x, wide):
    rows, lon = x.shape
    gap = jnp.zeros((rows, wide - lon - 2 * STEPS), x.dtype)
    return jnp.concatenate([x, x[:, :STEPS], gap, x[:, lon - STEPS :]], 1)


def kernel(
    cfg,
    first_hbm, currents_hbm, kappa_hbm, mask_hbm, cell_hbm, level_hbm, live_hbm, value_hbm, variance_hbm,
    out_ref,
    first_ref, currents_ref, kappa_ref, mask_ref, cell_ref, level_ref, live_ref, value_ref, variance_ref,
    states, leaving, raw_south, raw_north, from_south, from_north, v_south, v_north, k_south, k_north, mask_south, mask_north,
    coefs, units, own_all, picks, part, slice_parts, y_own, y_parts, z_own, z_parts, total, gram, mixed, landed,
    s_in, s_halo, r_halo, s_static, r_static, s_out, r_out, s_slice, r_slice, s_z, r_z, s_y, r_y,
    s_all, r_all, s_back, r_back,
):
    n_grid, n_mem, z_ring, levels, lon, wide, chunks = cfg
    y_ring = n_grid // z_ring
    own = 8 * chunks
    count = n_mem * own
    unit_wide = levels * wide // n_mem
    piece = unit_wide // 2
    pieces, pair = wide // piece, levels // 2
    full = wide - LANES
    grid = lax.axis_index("grid")
    mem = lax.axis_index("mem")
    y_at, z_at = grid // z_ring, lax.rem(grid, z_ring)
    has_north, has_south = grid < n_grid - 1, grid > 0

    def mem_peer(d):
        return lax.rem(mem + d, n_mem)

    def z_peer(d):
        return y_at * z_ring + lax.rem(z_at + d, z_ring)

    def y_peer(d):
        return lax.rem(y_at + d, y_ring) * z_ring + z_at

    local = [
        pltpu.make_async_copy(src, dst, s_in.at[index])
        for index, (src, dst) in enumerate(
            (
                (first_hbm, first_ref), (currents_hbm, currents_ref), (kappa_hbm, kappa_ref), (mask_hbm, mask_ref),
                (cell_hbm, cell_ref), (level_hbm, level_ref), (live_hbm, live_ref), (value_hbm, value_ref),
                (variance_hbm, variance_ref),
            )
        )
    ]
    for copy in local:
        copy.start()
    barrier = pltpu.get_barrier_semaphore()

    def greet(where):
        pl.semaphore_signal(barrier, inc=1, device_id=where, device_id_type=MESH)

    cross_north = jnp.logical_and(has_north, z_at == z_ring - 1)
    cross_south = jnp.logical_and(has_south, z_at == 0)

    @pl.when(cross_north)
    def _():
        greet({"grid": grid + 1})

    @pl.when(cross_south)
    def _():
        greet({"grid": grid - 1})

    for d in far_first(z_ring):
        greet({"grid": z_peer(d)})
    for d in far_first(y_ring):
        greet({"grid": y_peer(d)})
    for d in far_first(n_mem):
        greet({"mem": mem_peer(d)})
    greeted = z_ring + y_ring + n_mem - 3 + cross_north.astype(jnp.int32) + cross_south.astype(jnp.int32)
    pl.semaphore_wait(barrier, greeted)

    def remote(src, dst, send, recv, where):
        return pltpu.make_async_remote_copy(
            src_ref=src, dst_ref=dst, send_sem=send, recv_sem=recv, device_id=where, device_id_type=MESH
        )

    north, south = {"grid": grid + 1}, {"grid": grid - 1}

    def halo(step, chunk):
        if step == 0:
            rows = pl.ds(8 * chunk, 8)
            src, below, above = first_hbm.at[rows], raw_south.at[rows], raw_north.at[rows]
        else:
            at = (step - 1, chunk)
            src, below, above = leaving.at[at], from_south.at[at], from_north.at[at]
        if step < STEPS - 1:
            trips = [(step, src, below, above)]
        else:
            early = pl.ds(0, pair * full + LANES)
            late = pl.ds(pair * full + LANES, (levels - pair) * full)
            trips = [
                (step + index, src.at[:, lanes], below.at[:, lanes], above.at[:, lanes])
                for index, lanes in enumerate((early, late))
            ]
        return [
            (
                remote(src, below, s_halo.at[0, at, chunk], r_halo.at[0, at, chunk], north),
                remote(src, above, s_halo.at[1, at, chunk], r_halo.at[1, at, chunk], south),
            )
            for at, src, below, above in trips
        ]

    statics = (currents_hbm.at[1], kappa_hbm, mask_hbm)
    static_up = [
        remote(src, dst, s_static.at[0, index], r_static.at[0, index], north)
        for index, (src, dst) in enumerate(zip(statics, (v_south, k_south, mask_south)))
    ]
    static_down = [
        remote(src, dst, s_static.at[1, index], r_static.at[1, index], south)
        for index, (src, dst) in enumerate(zip(statics, (v_north, k_north, mask_north)))
    ]

    def start_halo(step, chunk):
        for up, down in halo(step, chunk):
            pl.when(has_north)(up.start)
            pl.when(has_south)(down.start)

    for copy in static_up:
        pl.when(has_north)(copy.start)
    for copy in static_down:
        pl.when(has_south)(copy.start)
    for chunk in range(chunks):
        start_halo(0, chunk)

    @pl.when(jnp.logical_not(has_south))
    def _():
        v_south[...] = jnp.zeros_like(v_south)
        k_south[...] = jnp.zeros_like(k_south)
        mask_south[...] = jnp.zeros_like(mask_south)
        raw_south[...] = jnp.zeros_like(raw_south)
        from_south[...] = jnp.zeros_like(from_south)

    @pl.when(jnp.logical_not(has_north))
    def _():
        v_north[...] = jnp.zeros_like(v_north)
        k_north[...] = jnp.zeros_like(k_north)
        mask_north[...] = jnp.zeros_like(mask_north)
        raw_north[...] = jnp.zeros_like(raw_north)
        from_north[...] = jnp.zeros_like(from_north)

    def first_rows(ref, chunk, level):
        return ring(ref[8 * chunk : 8 * chunk + 8, level, 0, :], wide)

    for copy in local:
        copy.wait()
    for chunk in range(chunks):
        for level in range(levels):
            states[0, chunk, level] = first_rows(first_ref, chunk, level)
    slots = cell_ref.shape[0]
    upper_pair = jnp.where(level_ref[...] >= pair, 1, 0)
    flat = (level_ref[...] - upper_pair * pair) * wide + cell_ref[...] - mem * piece
    place = jnp.where(jnp.logical_and(flat >= 0, flat < piece), flat + upper_pair * piece, -1).reshape(1, slots)
    inside = place >= 0
    live = lax.broadcasted_iota(jnp.int32, (1, slots), 1) < live_ref[0]
    weight = jnp.where(jnp.logical_and(inside, live), 1.0 / jnp.sqrt(variance_ref[...].reshape(1, slots)), 0.0)
    picks[...] = jnp.where(
        lax.broadcasted_iota(jnp.int32, (unit_wide, slots), 0) == place, 1.0, 0.0
    ).astype(jnp.bfloat16)

    def rows_of(ref):
        return ring(ref[:, 0, :], wide)

    def sea_of(ref):
        return jnp.broadcast_to(ring(ref[...].astype(jnp.float32), wide), (levels, wide))

    zonal, velocity = ring(currents_ref[0, :, 0, :], wide), ring(currents_ref[1, :, 0, :], wide)
    kappa, sea = rows_of(kappa_ref), sea_of(mask_ref)
    a_east, b_east = faces(
        zonal, pltpu.roll(zonal, wide - 1, 1), kappa, pltpu.roll(kappa, wide - 1, 1), sea, pltpu.roll(sea, wide - 1, 1)
    )
    a_west, b_west = pltpu.roll(a_east, 1, 1), pltpu.roll(b_east, 1, 1)

    for copy in static_up:
        pl.when(has_south)(copy.wait_recv)
    for copy in static_down:
        pl.when(has_north)(copy.wait_recv)
    a_north, b_north = faces(velocity, rows_of(v_north), kappa, rows_of(k_north), sea, sea_of(mask_north))
    a_south, b_south = faces(rows_of(v_south), velocity, rows_of(k_south), kappa, sea_of(mask_south), sea)
    depth = lax.broadcasted_iota(jnp.int32, (levels, wide), 0)
    vertical = VERTICAL_MIX * sea
    borders = jnp.where(jnp.logical_or(depth == 0, depth == levels - 1), 1.0, 2.0)
    relax = jnp.where(depth == 0, 1.0 - SURFACE_RELAX * sea, 1.0)
    centre = 1.0 - a_east + b_west - a_north + b_south - borders * vertical
    parts = (centre, -b_east, a_west, -b_north, a_south, vertical, AGE_RATE * sea)
    for index, values in enumerate(parts):
        values = values * relax
        for level in range(levels):
            coefs[level, index] = jnp.broadcast_to(values[level : level + 1], (8, wide))

    def landing(chunk, which):
        return pl.ds(pl.multiple_of(mem * own + 8 * chunk, 8), 8), pl.ds(which * piece, piece)

    def sent(chunk, which):
        return [
            remote(
                units.at[mem_peer(d), chunk, which], own_all.at[landing(chunk, which)],
                s_out.at[d - 1, chunk, which], r_out.at[d - 1, chunk, which], {"mem": mem_peer(d)},
            )
            for d in far_first(n_mem)
        ]

    last_lanes = lon - full
    tail_lane = lax.broadcasted_iota(jnp.int32, (8, LANES), 1)
    for step in range(STEPS):
        for chunk in range(chunks):
            arriving = halo(step, chunk)
            for level in range(levels):
                if level % (levels // len(arriving)) == 0:
                    up, down = arriving[level * len(arriving) // levels]
                    pl.when(has_south)(up.wait_recv)
                    pl.when(has_north)(down.wait_recv)

                def at(which):
                    return states[step, chunk, which]

                if step == 0:
                    above, below = first_rows(raw_north, chunk, level), first_rows(raw_south, chunk, level)
                else:
                    above = spread_row(from_north.at[step - 1, chunk], level, levels, lon, wide)
                    below = spread_row(from_south.at[step - 1, chunk], level, levels, lon, wide)
                here = at(level)
                around = at(level - 1) if level > 0 else 0.0
                if level < levels - 1:
                    around = around + at(level + 1)
                result = (
                    coefs[level, 0] * here
                    + coefs[level, 1] * pltpu.roll(here, wide - 1, 1)
                    + coefs[level, 2] * pltpu.roll(here, 1, 1)
                    + coefs[level, 3] * above
                    + coefs[level, 4] * below
                    + coefs[level, 5] * around
                    + coefs[level, 6]
                )
                if step < STEPS - 1:
                    states[step + 1, chunk, level] = result
                    start = body_start(level, levels, full)
                    leaving[step, chunk, :, start : start + full] = result[:, :full]
                    moved = result[:, full:] if level == 0 else pltpu.roll(result[:, full:], level * last_lanes, 1)
                    packed = moved if level == 0 else jnp.where(tail_lane < level * last_lanes, packed, moved)
                else:
                    for index in range(pieces):
                        units[level % pair * pieces + index, chunk, level // pair] = result[
                            :, index * piece : (index + 1) * piece
                        ]
                    if level % pair == pair - 1:
                        for copy in sent(chunk, level // pair):
                            copy.start()
                        rows, lanes = landing(chunk, level // pair)
                        own_all[rows, lanes] = units[mem, chunk, level // pair]
            if step < STEPS - 1:
                leaving[step, chunk, :, pair * full : pair * full + LANES] = packed
                start_halo(step + 1, chunk)

    def exchange(src_of, dst_of, send, recv, peers, axis, peer):
        return [remote(src_of(d), dst_of(d), send.at[d - 1], recv.at[d - 1], {axis: peer(d)}) for d in far_first(peers)]

    outs = [copy for chunk in range(chunks) for which in range(2) for copy in sent(chunk, which)]
    for copy in outs:
        copy.wait_recv()

    fields = own_all[...]
    high = fields.astype(jnp.bfloat16)
    rest = fields - high.astype(jnp.float32)
    middle = rest.astype(jnp.bfloat16)
    low = (rest - middle.astype(jnp.float32)).astype(jnp.bfloat16)
    seen = (
        jnp.dot(high, picks[...], preferred_element_type=jnp.float32)
        + jnp.dot(middle, picks[...], preferred_element_type=jnp.float32)
        + jnp.dot(low, picks[...], preferred_element_type=jnp.float32)
    )
    root = math.sqrt(count)
    inner = 1.0 / (count * (1.0 / root + 1.0))
    last = lax.broadcasted_iota(jnp.int32, (count, slots), 0) == count - 1
    everyone = jnp.sum(seen, axis=0, keepdims=True)
    final = seen[count - 1 : count]
    shared = -inner * (everyone - final) - final / root
    stacked = jnp.where(last, value_ref[...].reshape(1, slots) - everyone / count, seen + shared) * weight
    folded, diagonal = fold_square(lax.dot_general(
        stacked, stacked, (((1,), (1,)), ((), ())), precision=HIGHEST, preferred_element_type=jnp.float32
    ), count)
    share = count // 2 // n_mem
    for index in range(n_mem):
        part[index, :share] = folded[index * share : (index + 1) * share]
        part[index, share:] = diagonal

    slices = exchange(lambda d: part.at[mem_peer(d)], lambda d: slice_parts.at[d - 1], s_slice, r_slice, n_mem, "mem", mem_peer)
    for copy in slices:
        copy.start()
    for copy in slices:
        copy.wait_recv()
    z_own[...] = part[mem] + jnp.sum(slice_parts[...], axis=0)
    along_z = exchange(lambda d: z_own, lambda d: z_parts.at[d - 1], s_z, r_z, z_ring, "grid", z_peer)
    for copy in along_z:
        copy.start()
    for copy in along_z:
        copy.wait_recv()
    y_own[...] = z_own[...] + jnp.sum(z_parts[...], axis=0)
    along_y = exchange(lambda d: y_own, lambda d: y_parts.at[d - 1], s_y, r_y, y_ring, "grid", y_peer)
    for copy in along_y:
        copy.start()
    for copy in along_y:
        copy.wait_recv()
    total[...] = y_own[...] + jnp.sum(y_parts[...], axis=0)
    gathered = exchange(lambda d: total, lambda d: gram.at[mem], s_all, r_all, n_mem, "mem", mem_peer)
    for copy in gathered:
        copy.start()
    gram[mem] = total[...]
    for copy in gathered:
        copy.wait_recv()

    folded = jnp.concatenate([gram[index, :share] for index in range(n_mem)], 0)
    inverse = factor_inverse(unfold_square(folded, gram[0, share:], count), count)
    square_lane = lax.broadcasted_iota(jnp.int32, (count, count), 1)
    square_row = lax.broadcasted_iota(jnp.int32, (count, count), 0)
    leading = jnp.where(square_lane < count - 1, inverse, 0.0)
    across = jnp.sum(leading, axis=1, keepdims=True)
    turned = jnp.where(square_lane == count - 1, -across / root, leading - inner * across)
    shift = -turned[count - 1 : count] / inverse[count - 1 : count, count - 1 : count]
    kept = jnp.where(square_row < count - 1, turned, 0.0)
    down_sum = jnp.sum(kept, axis=0, keepdims=True)
    spread = jnp.where(square_row == count - 1, -down_sum / root, kept - inner * down_sum)
    mixing = 1.0 / count + shift + math.sqrt(count - 1) * spread
    mixed[...] = jnp.dot(mixing, own_all[...], precision=HIGHEST).reshape(n_mem, own, unit_wide)
    back = exchange(lambda d: mixed.at[mem_peer(d)], lambda d: landed.at[mem], s_back, r_back, n_mem, "mem", mem_peer)
    for copy in back:
        copy.start()
    landed[mem] = mixed[mem]
    for copy in back:
        copy.wait_recv()
    for member in range(n_mem):
        for which in range(2):
            lane = member % pieces * piece
            count_here = min(piece, lon - lane)
            out_ref[which * pair + member // pieces, :, lane : lane + count_here] = landed[
                member, :, which * piece : which * piece + count_here
            ]

    for step in range(STEPS):
        for chunk in range(chunks):
            for up, down in halo(step, chunk):
                pl.when(has_north)(up.wait_send)
                pl.when(has_south)(down.wait_send)
    for copy in static_up:
        pl.when(has_north)(copy.wait_send)
    for copy in static_down:
        pl.when(has_south)(copy.wait_send)
    for copy in outs + slices + along_z + along_y + gathered + back:
        copy.wait_send()


def per_device(
    n_grid, n_mem, z_ring,
    background_elapsed_years, currents, diffusivity, sea_mask, observed_cell, measured_layer_number, live_counts,
    observed_value, error_variance,
):
    own, levels, _, lon = background_elapsed_years.shape
    chunks, slots = own // 8, observed_cell.shape[0]
    halves = n_mem // levels
    block = LANES * halves
    wide = -(-(lon + 2 * STEPS) // block) * block
    unit_wide = levels * wide // n_mem
    y_ring = n_grid // z_ring
    count = own * n_mem
    f32 = jnp.float32
    dma = pltpu.SemaphoreType.DMA
    packed_shape = (STEPS - 1, chunks, 8, levels * (wide - LANES) + LANES)
    halo_shape = (STEPS, chunks, levels, 8, wide)
    i32 = jnp.int32
    scratch = [
        pltpu.VMEM((own, levels, 1, lon), f32),
        pltpu.VMEM((2, levels, 1, lon), f32),
        pltpu.VMEM((levels, 1, lon), f32),
        pltpu.VMEM((1, lon), i32),
        pltpu.VMEM((slots,), i32),
        pltpu.VMEM((slots,), i32),
        pltpu.SMEM((1,), i32),
        pltpu.VMEM((slots,), f32),
        pltpu.VMEM((slots,), f32),
        pltpu.VMEM(halo_shape, f32),
        pltpu.VMEM(packed_shape, f32),
        pltpu.VMEM((own, levels, 1, lon), f32),
        pltpu.VMEM((own, levels, 1, lon), f32),
        pltpu.VMEM(packed_shape, f32),
        pltpu.VMEM(packed_shape, f32),
        pltpu.VMEM((levels, 1, lon), f32),
        pltpu.VMEM((levels, 1, lon), f32),
        pltpu.VMEM((levels, 1, lon), f32),
        pltpu.VMEM((levels, 1, lon), f32),
        pltpu.VMEM((1, lon), i32),
        pltpu.VMEM((1, lon), i32),
        pltpu.VMEM((levels, 7, 8, wide), f32),
        pltpu.VMEM((n_mem, chunks, 2, 8, unit_wide // 2), f32),
        pltpu.VMEM((count, unit_wide), f32),
        pltpu.VMEM((unit_wide, slots), jnp.bfloat16),
        pltpu.VMEM((n_mem, count // 2 // n_mem + 1, count), f32),
        pltpu.VMEM((n_mem - 1, count // 2 // n_mem + 1, count), f32),
        pltpu.VMEM((count // 2 // n_mem + 1, count), f32),
        pltpu.VMEM((y_ring - 1, count // 2 // n_mem + 1, count), f32),
        pltpu.VMEM((count // 2 // n_mem + 1, count), f32),
        pltpu.VMEM((z_ring - 1, count // 2 // n_mem + 1, count), f32),
        pltpu.VMEM((count // 2 // n_mem + 1, count), f32),
        pltpu.VMEM((n_mem, count // 2 // n_mem + 1, count), f32),
        pltpu.VMEM((n_mem, own, unit_wide), f32),
        pltpu.VMEM((n_mem, own, unit_wide), f32),
    ]
    semaphores = [
        dma((9,)),
        dma((2, STEPS + 1, chunks)), dma((2, STEPS + 1, chunks)),
        dma((2, 3)), dma((2, 3)),
        dma((n_mem - 1, chunks, 2)), dma((n_mem - 1, chunks, 2)),
        dma((n_mem - 1,)), dma((n_mem - 1,)),
        dma((z_ring - 1,)), dma((z_ring - 1,)),
        dma((y_ring - 1,)), dma((y_ring - 1,)),
        dma((n_mem - 1,)), dma((n_mem - 1,)),
        dma((n_mem - 1,)), dma((n_mem - 1,)),
    ]
    result = pl.pallas_call(
        functools.partial(kernel, (n_grid, n_mem, z_ring, levels, lon, wide, chunks)),
        out_shape=pltpu.VMEM((levels, own, lon), f32),
        in_specs=[pl.BlockSpec(memory_space=pltpu.HBM)] * 9,
        out_specs=pl.BlockSpec(memory_space=pltpu.VMEM),
        scratch_shapes=scratch + semaphores,
        compiler_params=pltpu.CompilerParams(
            collective_id=0, has_side_effects=True, vmem_limit_bytes=60 * 1024 * 1024
        ),
    )(
        background_elapsed_years, currents, diffusivity, sea_mask, observed_cell, measured_layer_number, live_counts,
        observed_value, error_variance,
    )
    return result.transpose(1, 0, 2)[:, :, None, :]


def solution(mesh):
    placed = (
        P("mem", None, "grid", None),
        P(None, None, "grid", None),
        P(None, "grid", None),
        P("grid", None),
        P("grid"),
        P("grid"),
        P("grid"),
        P("grid"),
        P("grid"),
    )
    return jax.shard_map(
        functools.partial(per_device, mesh.shape["grid"], mesh.shape["mem"], Z_RING),
        mesh=mesh,
        in_specs=placed,
        out_specs=P("mem", None, "grid", None),
        check_vma=False,
    )
```

```python
import functools
import math

import jax
import jax.numpy as jnp
from jax import lax
from jax.experimental import pallas as pl
from jax.experimental.pallas import tpu as pltpu
from jax.sharding import PartitionSpec as P

STEPS = 4
Z_RING = 12
LANES = 128
PANEL = 64
VERTICAL_MIX = 0.05
AGE_RATE = 0.25
SURFACE_RELAX = 0.5
HIGHEST = lax.Precision.HIGHEST
MESH = pl.DeviceIdType.MESH


def faces(speed_a, speed_b, kappa_a, kappa_b, sea_a, sea_b):
    speed = 0.5 * (speed_a + speed_b)
    kappa = 0.5 * (kappa_a + kappa_b)
    both = sea_a * sea_b
    return both * (jnp.maximum(speed, 0.0) + kappa), both * (jnp.minimum(speed, 0.0) - kappa)


def factor_inverse(gram, count):
    panel = min(PANEL, count)
    wide_row = lax.broadcasted_iota(jnp.int32, (panel, count), 0)
    lane = lax.broadcasted_iota(jnp.int32, (panel, count), 1)
    row = lax.broadcasted_iota(jnp.int32, (8, count), 0)
    full_row = lax.broadcasted_iota(jnp.int32, (count, count), 0)
    full_lane = lax.broadcasted_iota(jnp.int32, (count, count), 1)
    left = gram + jnp.where(full_row == full_lane, float(count - 1), 0.0)
    right = jnp.where(full_row == full_lane, 1.0, 0.0)
    done = []
    for first in range(0, count, panel):
        a_rest, e_rest = left[:panel], right[:panel]
        a_done, e_done = [], []
        for base in range(first, first + panel, 8):
            a, e, a_rest, e_rest = a_rest[:8], e_rest[:8], a_rest[8:], e_rest[8:]
            columns = [jnp.broadcast_to(a[:, base + j : base + j + 1], (8, count)) for j in range(8)]
            scales = []
            for k in range(0, 8, 2):
                now, later = columns[k], columns[k + 1]
                p, q, r = now[k : k + 1], now[k + 1 : k + 2], later[k + 1 : k + 2]
                per_pair, per_p = 1.0 / (p * r - q * q), 1.0 / p
                below_now, below_later = jnp.where(row > k + 1, now, 0.0), jnp.where(row > k + 1, later, 0.0)
                first_factor = (below_now * r - below_later * q) * per_pair
                later_factor = (below_later * p - below_now * q) * per_pair
                first_factor = jnp.where(row == k + 1, q * per_p, first_factor)
                for j in range(k + 2, 8):
                    at = columns[j]
                    columns[j] = at - (first_factor * at[k : k + 1] + later_factor * at[k + 1 : k + 2])
                a = a - (first_factor * a[k : k + 1] + later_factor * a[k + 1 : k + 2])
                e = e - (first_factor * e[k : k + 1] + later_factor * e[k + 1 : k + 2])
                scales += [per_p, per_pair * p]
            a_done.append(a)
            e_done.append(e)
            rows = first + panel - base - 8
            if rows:
                lower = [jnp.broadcast_to(a_rest[:, base + j : base + j + 1], (rows, count)) for j in range(8)]
                for k in range(8):
                    factor = lower[k] * scales[k]
                    for j in range(k + 1, 8):
                        lower[j] = lower[j] - factor * columns[j][k : k + 1]
                    a_rest = a_rest - factor * a[k : k + 1]
                    e_rest = e_rest - factor * e[k : k + 1]
        a, e = jnp.concatenate(a_done, 0), jnp.concatenate(e_done, 0)
        pivots = jnp.sum(jnp.where(lane == wide_row + first, a, 0.0), axis=1, keepdims=True)
        root = lax.rsqrt(pivots)
        a, e = a * root, e * root
        done.append(e)
        if first + panel < count:
            turned = jnp.transpose(a)[first + panel :]
            left = left[panel:] - jnp.dot(turned, a, precision=HIGHEST)
            right = right[panel:] - jnp.dot(turned, e, precision=HIGHEST)
    return jnp.concatenate(done, 0)


def fold_square(square, count):
    half = count // 2
    row = lax.broadcasted_iota(jnp.int32, (half, count), 0)
    lane = lax.broadcasted_iota(jnp.int32, (half, count), 1)
    upper, lower = pltpu.roll(square[:half], half, 1), square[half:]
    folded = jnp.where(jnp.logical_or(lane < half, row <= lane - half), upper, lower)
    return folded, jnp.sum(jnp.where(row == lane - half, lower, 0.0), axis=0, keepdims=True)


def unfold_square(folded, diagonal, count):
    half = count // 2
    row = lax.broadcasted_iota(jnp.int32, (count, count), 0)
    lane = lax.broadcasted_iota(jnp.int32, (count, count), 1)
    here = jnp.concatenate([pltpu.roll(folded, half, 1), folded], 0)
    turned = jnp.transpose(here)
    top = jnp.logical_and(row < half, row <= lane)
    bottom = jnp.logical_and(lane >= half, row > lane)
    square = jnp.where(jnp.logical_or(top, bottom), here, turned)
    return jnp.where(jnp.logical_and(row == lane, row >= half), diagonal, square)


def far_first(peers):
    return sorted(range(1, peers), key=lambda d: -min(d, peers - d))


def spread_row(flat, level, levels, lon, wide):
    full, last = wide - LANES, lon - (wide - LANES)
    body, packed = flat[:, level * full : (level + 1) * full], flat[:, levels * full :]
    lane = lax.broadcasted_iota(jnp.int32, (8, LANES), 1)
    ending = packed if level == 0 else pltpu.roll(packed, LANES - level * last, 1)
    opening, closing = pltpu.roll(body[:, :LANES], last, 1), pltpu.roll(ending, LANES - last, 1)
    tail = jnp.where(lane < last + STEPS, jnp.where(lane < last, ending, opening), 0.0)
    return jnp.concatenate([body, jnp.where(lane >= LANES - STEPS, closing, tail)], 1)


def ring(x, wide):
    rows, lon = x.shape
    gap = jnp.zeros((rows, wide - lon - 2 * STEPS), x.dtype)
    return jnp.concatenate([x, x[:, :STEPS], gap, x[:, lon - STEPS :]], 1)


def kernel(
    cfg,
    first_hbm, currents_hbm, kappa_hbm, mask_hbm, cell_hbm, level_hbm, live_hbm, value_hbm, variance_hbm,
    out_ref,
    first_ref, currents_ref, kappa_ref, mask_ref, cell_ref, level_ref, live_ref, value_ref, variance_ref,
    states, leaving, raw_south, raw_north, from_south, from_north, v_south, v_north, k_south, k_north, mask_south, mask_north,
    coefs, units, own_all, picks, part, slice_parts, y_own, y_parts, z_own, z_parts, total, gram, mixed, landed,
    s_in, s_halo, r_halo, s_static, r_static, s_out, r_out, s_slice, r_slice, s_z, r_z, s_y, r_y,
    s_all, r_all, s_back, r_back,
):
    n_grid, n_mem, z_ring, levels, lon, wide, chunks = cfg
    y_ring = n_grid // z_ring
    own = 8 * chunks
    count = n_mem * own
    unit_wide = levels * wide // n_mem
    halves = n_mem // levels
    grid = lax.axis_index("grid")
    mem = lax.axis_index("mem")
    y_at, z_at = grid // z_ring, lax.rem(grid, z_ring)
    has_north, has_south = grid < n_grid - 1, grid > 0

    def mem_peer(d):
        return lax.rem(mem + d, n_mem)

    def z_peer(d):
        return y_at * z_ring + lax.rem(z_at + d, z_ring)

    def y_peer(d):
        return lax.rem(y_at + d, y_ring) * z_ring + z_at

    local = [
        pltpu.make_async_copy(src, dst, s_in.at[index])
        for index, (src, dst) in enumerate(
            (
                (first_hbm, first_ref), (currents_hbm, currents_ref), (kappa_hbm, kappa_ref), (mask_hbm, mask_ref),
                (cell_hbm, cell_ref), (level_hbm, level_ref), (live_hbm, live_ref), (value_hbm, value_ref),
                (variance_hbm, variance_ref),
            )
        )
    ]
    for copy in local:
        copy.start()
    barrier = pltpu.get_barrier_semaphore()

    def greet(where):
        pl.semaphore_signal(barrier, inc=1, device_id=where, device_id_type=MESH)

    cross_north = jnp.logical_and(has_north, z_at == z_ring - 1)
    cross_south = jnp.logical_and(has_south, z_at == 0)

    @pl.when(cross_north)
    def _():
        greet({"grid": grid + 1})

    @pl.when(cross_south)
    def _():
        greet({"grid": grid - 1})

    for d in far_first(z_ring):
        greet({"grid": z_peer(d)})
    for d in far_first(y_ring):
        greet({"grid": y_peer(d)})
    for d in far_first(n_mem):
        greet({"mem": mem_peer(d)})
    greeted = z_ring + y_ring + n_mem - 3 + cross_north.astype(jnp.int32) + cross_south.astype(jnp.int32)
    pl.semaphore_wait(barrier, greeted)

    def remote(src, dst, send, recv, where):
        return pltpu.make_async_remote_copy(
            src_ref=src, dst_ref=dst, send_sem=send, recv_sem=recv, device_id=where, device_id_type=MESH
        )

    north, south = {"grid": grid + 1}, {"grid": grid - 1}

    def halo(step, chunk):
        if step == 0:
            rows = pl.ds(8 * chunk, 8)
            src, below, above = first_hbm.at[rows], raw_south.at[rows], raw_north.at[rows]
        else:
            at = (step - 1, chunk)
            src, below, above = leaving.at[at], from_south.at[at], from_north.at[at]
        up = remote(src, below, s_halo.at[0, step, chunk], r_halo.at[0, step, chunk], north)
        down = remote(src, above, s_halo.at[1, step, chunk], r_halo.at[1, step, chunk], south)
        return up, down

    statics = (currents_hbm.at[1], kappa_hbm, mask_hbm)
    static_up = [
        remote(src, dst, s_static.at[0, index], r_static.at[0, index], north)
        for index, (src, dst) in enumerate(zip(statics, (v_south, k_south, mask_south)))
    ]
    static_down = [
        remote(src, dst, s_static.at[1, index], r_static.at[1, index], south)
        for index, (src, dst) in enumerate(zip(statics, (v_north, k_north, mask_north)))
    ]

    def start_halo(step, chunk):
        up, down = halo(step, chunk)
        pl.when(has_north)(up.start)
        pl.when(has_south)(down.start)

    for copy in static_up:
        pl.when(has_north)(copy.start)
    for copy in static_down:
        pl.when(has_south)(copy.start)
    for chunk in range(chunks):
        start_halo(0, chunk)

    @pl.when(jnp.logical_not(has_south))
    def _():
        v_south[...] = jnp.zeros_like(v_south)
        k_south[...] = jnp.zeros_like(k_south)
        mask_south[...] = jnp.zeros_like(mask_south)
        raw_south[...] = jnp.zeros_like(raw_south)
        from_south[...] = jnp.zeros_like(from_south)

    @pl.when(jnp.logical_not(has_north))
    def _():
        v_north[...] = jnp.zeros_like(v_north)
        k_north[...] = jnp.zeros_like(k_north)
        mask_north[...] = jnp.zeros_like(mask_north)
        raw_north[...] = jnp.zeros_like(raw_north)
        from_north[...] = jnp.zeros_like(from_north)

    def first_rows(ref, chunk, level):
        return ring(ref[8 * chunk : 8 * chunk + 8, level, 0, :], wide)

    for copy in local:
        copy.wait()
    for chunk in range(chunks):
        for level in range(levels):
            states[0, chunk, level] = first_rows(first_ref, chunk, level)
    slots = cell_ref.shape[0]
    place = (level_ref[...] * wide + cell_ref[...]).reshape(1, slots) - mem * unit_wide
    inside = jnp.logical_and(place >= 0, place < unit_wide)
    live = lax.broadcasted_iota(jnp.int32, (1, slots), 1) < live_ref[0]
    weight = jnp.where(jnp.logical_and(inside, live), 1.0 / jnp.sqrt(variance_ref[...].reshape(1, slots)), 0.0)
    picks[...] = jnp.where(
        lax.broadcasted_iota(jnp.int32, (unit_wide, slots), 0) == place, 1.0, 0.0
    ).astype(jnp.bfloat16)

    def rows_of(ref):
        return ring(ref[:, 0, :], wide)

    def sea_of(ref):
        return jnp.broadcast_to(ring(ref[...].astype(jnp.float32), wide), (levels, wide))

    zonal, velocity = ring(currents_ref[0, :, 0, :], wide), ring(currents_ref[1, :, 0, :], wide)
    kappa, sea = rows_of(kappa_ref), sea_of(mask_ref)
    a_east, b_east = faces(
        zonal, pltpu.roll(zonal, wide - 1, 1), kappa, pltpu.roll(kappa, wide - 1, 1), sea, pltpu.roll(sea, wide - 1, 1)
    )
    a_west, b_west = pltpu.roll(a_east, 1, 1), pltpu.roll(b_east, 1, 1)

    for copy in static_up:
        pl.when(has_south)(copy.wait_recv)
    for copy in static_down:
        pl.when(has_north)(copy.wait_recv)
    a_north, b_north = faces(velocity, rows_of(v_north), kappa, rows_of(k_north), sea, sea_of(mask_north))
    a_south, b_south = faces(rows_of(v_south), velocity, rows_of(k_south), kappa, sea_of(mask_south), sea)
    depth = lax.broadcasted_iota(jnp.int32, (levels, wide), 0)
    vertical = VERTICAL_MIX * sea
    borders = jnp.where(jnp.logical_or(depth == 0, depth == levels - 1), 1.0, 2.0)
    relax = jnp.where(depth == 0, 1.0 - SURFACE_RELAX * sea, 1.0)
    centre = 1.0 - a_east + b_west - a_north + b_south - borders * vertical
    parts = (centre, -b_east, a_west, -b_north, a_south, vertical, AGE_RATE * sea)
    for index, values in enumerate(parts):
        values = values * relax
        for level in range(levels):
            coefs[level, index] = jnp.broadcast_to(values[level : level + 1], (8, wide))

    full = wide - LANES
    last_lanes = lon - full
    tail_lane = lax.broadcasted_iota(jnp.int32, (8, LANES), 1)
    for step in range(STEPS):
        for chunk in range(chunks):
            up, down = halo(step, chunk)
            pl.when(has_south)(up.wait_recv)
            pl.when(has_north)(down.wait_recv)
            for level in range(levels):
                def at(which):
                    return states[step, chunk, which]

                if step == 0:
                    above, below = first_rows(raw_north, chunk, level), first_rows(raw_south, chunk, level)
                else:
                    above = spread_row(from_north.at[step - 1, chunk], level, levels, lon, wide)
                    below = spread_row(from_south.at[step - 1, chunk], level, levels, lon, wide)
                here = at(level)
                around = at(level - 1) if level > 0 else 0.0
                if level < levels - 1:
                    around = around + at(level + 1)
                result = (
                    coefs[level, 0] * here
                    + coefs[level, 1] * pltpu.roll(here, wide - 1, 1)
                    + coefs[level, 2] * pltpu.roll(here, 1, 1)
                    + coefs[level, 3] * above
                    + coefs[level, 4] * below
                    + coefs[level, 5] * around
                    + coefs[level, 6]
                )
                if step < STEPS - 1:
                    states[step + 1, chunk, level] = result
                    leaving[step, chunk, :, level * full : (level + 1) * full] = result[:, :full]
                    moved = result[:, full:] if level == 0 else pltpu.roll(result[:, full:], level * last_lanes, 1)
                    packed = moved if level == 0 else jnp.where(tail_lane < level * last_lanes, packed, moved)
                else:
                    for half in range(halves):
                        units[level * halves + half, chunk] = result[:, half * unit_wide : (half + 1) * unit_wide]
            if step < STEPS - 1:
                leaving[step, chunk, :, levels * full :] = packed
                start_halo(step + 1, chunk)
            else:
                rows = pl.ds(pl.multiple_of(mem * own + 8 * chunk, 8), 8)
                for d in far_first(n_mem):
                    remote(
                        units.at[mem_peer(d), chunk], own_all.at[rows], s_out.at[d - 1, chunk], r_out.at[d - 1, chunk],
                        {"mem": mem_peer(d)},
                    ).start()
                own_all[rows, :] = units[mem, chunk]

    def exchange(src_of, dst_of, send, recv, peers, axis, peer):
        return [remote(src_of(d), dst_of(d), send.at[d - 1], recv.at[d - 1], {axis: peer(d)}) for d in far_first(peers)]

    outs = [
        remote(
            units.at[mem_peer(d), chunk],
            own_all.at[pl.ds(pl.multiple_of(mem * own + 8 * chunk, 8), 8)],
            s_out.at[d - 1, chunk], r_out.at[d - 1, chunk], {"mem": mem_peer(d)},
        )
        for d in range(1, n_mem)
        for chunk in range(chunks)
    ]
    for copy in outs:
        copy.wait_recv()

    fields = own_all[...]
    high = fields.astype(jnp.bfloat16)
    rest = fields - high.astype(jnp.float32)
    middle = rest.astype(jnp.bfloat16)
    low = (rest - middle.astype(jnp.float32)).astype(jnp.bfloat16)
    seen = (
        jnp.dot(high, picks[...], preferred_element_type=jnp.float32)
        + jnp.dot(middle, picks[...], preferred_element_type=jnp.float32)
        + jnp.dot(low, picks[...], preferred_element_type=jnp.float32)
    )
    root = math.sqrt(count)
    inner = 1.0 / (count * (1.0 / root + 1.0))
    last = lax.broadcasted_iota(jnp.int32, (count, slots), 0) == count - 1
    everyone = jnp.sum(seen, axis=0, keepdims=True)
    final = seen[count - 1 : count]
    shared = -inner * (everyone - final) - final / root
    stacked = jnp.where(last, value_ref[...].reshape(1, slots) - everyone / count, seen + shared) * weight
    folded, diagonal = fold_square(lax.dot_general(
        stacked, stacked, (((1,), (1,)), ((), ())), precision=HIGHEST, preferred_element_type=jnp.float32
    ), count)
    share = count // 2 // n_mem
    for index in range(n_mem):
        part[index, :share] = folded[index * share : (index + 1) * share]
        part[index, share:] = diagonal

    slices = exchange(lambda d: part.at[mem_peer(d)], lambda d: slice_parts.at[d - 1], s_slice, r_slice, n_mem, "mem", mem_peer)
    for copy in slices:
        copy.start()
    for copy in slices:
        copy.wait_recv()
    z_own[...] = part[mem] + jnp.sum(slice_parts[...], axis=0)
    along_z = exchange(lambda d: z_own, lambda d: z_parts.at[d - 1], s_z, r_z, z_ring, "grid", z_peer)
    for copy in along_z:
        copy.start()
    for copy in along_z:
        copy.wait_recv()
    y_own[...] = z_own[...] + jnp.sum(z_parts[...], axis=0)
    along_y = exchange(lambda d: y_own, lambda d: y_parts.at[d - 1], s_y, r_y, y_ring, "grid", y_peer)
    for copy in along_y:
        copy.start()
    for copy in along_y:
        copy.wait_recv()
    total[...] = y_own[...] + jnp.sum(y_parts[...], axis=0)
    gathered = exchange(lambda d: total, lambda d: gram.at[mem], s_all, r_all, n_mem, "mem", mem_peer)
    for copy in gathered:
        copy.start()
    gram[mem] = total[...]
    for copy in gathered:
        copy.wait_recv()

    folded = jnp.concatenate([gram[index, :share] for index in range(n_mem)], 0)
    inverse = factor_inverse(unfold_square(folded, gram[0, share:], count), count)
    square_lane = lax.broadcasted_iota(jnp.int32, (count, count), 1)
    square_row = lax.broadcasted_iota(jnp.int32, (count, count), 0)
    leading = jnp.where(square_lane < count - 1, inverse, 0.0)
    across = jnp.sum(leading, axis=1, keepdims=True)
    turned = jnp.where(square_lane == count - 1, -across / root, leading - inner * across)
    shift = -turned[count - 1 : count] / inverse[count - 1 : count, count - 1 : count]
    kept = jnp.where(square_row < count - 1, turned, 0.0)
    down_sum = jnp.sum(kept, axis=0, keepdims=True)
    spread = jnp.where(square_row == count - 1, -down_sum / root, kept - inner * down_sum)
    mixing = 1.0 / count + shift + math.sqrt(count - 1) * spread
    mixed[...] = jnp.dot(mixing, own_all[...], precision=HIGHEST).reshape(n_mem, own, unit_wide)
    mine = (
        mem // halves,
        slice(None),
        pl.ds(pl.multiple_of(lax.rem(mem, halves) * unit_wide, LANES), unit_wide),
    )
    back = exchange(lambda d: mixed.at[mem_peer(d)], lambda d: landed.at[mine], s_back, r_back, n_mem, "mem", mem_peer)
    for copy in back:
        copy.start()
    landed[mine] = mixed[mem]
    for copy in back:
        copy.wait_recv()
    for level in range(levels):
        out_ref[level] = landed[level][:, : out_ref.shape[2]]

    for step in range(STEPS):
        for chunk in range(chunks):
            up, down = halo(step, chunk)
            pl.when(has_north)(up.wait_send)
            pl.when(has_south)(down.wait_send)
    for copy in static_up:
        pl.when(has_north)(copy.wait_send)
    for copy in static_down:
        pl.when(has_south)(copy.wait_send)
    for copy in outs + slices + along_z + along_y + gathered + back:
        copy.wait_send()


def per_device(
    n_grid, n_mem, z_ring,
    background_elapsed_years, currents, diffusivity, sea_mask, observed_cell, measured_layer_number, live_counts,
    observed_value, error_variance,
):
    own, levels, _, lon = background_elapsed_years.shape
    chunks, slots = own // 8, observed_cell.shape[0]
    halves = n_mem // levels
    block = LANES * halves
    wide = -(-(lon + 2 * STEPS) // block) * block
    unit_wide = wide // halves
    y_ring = n_grid // z_ring
    count = own * n_mem
    f32 = jnp.float32
    dma = pltpu.SemaphoreType.DMA
    packed_shape = (STEPS - 1, chunks, 8, levels * (wide - LANES) + LANES)
    halo_shape = (STEPS, chunks, levels, 8, wide)
    i32 = jnp.int32
    scratch = [
        pltpu.VMEM((own, levels, 1, lon), f32),
        pltpu.VMEM((2, levels, 1, lon), f32),
        pltpu.VMEM((levels, 1, lon), f32),
        pltpu.VMEM((1, lon), i32),
        pltpu.VMEM((slots,), i32),
        pltpu.VMEM((slots,), i32),
        pltpu.SMEM((1,), i32),
        pltpu.VMEM((slots,), f32),
        pltpu.VMEM((slots,), f32),
        pltpu.VMEM(halo_shape, f32),
        pltpu.VMEM(packed_shape, f32),
        pltpu.VMEM((own, levels, 1, lon), f32),
        pltpu.VMEM((own, levels, 1, lon), f32),
        pltpu.VMEM(packed_shape, f32),
        pltpu.VMEM(packed_shape, f32),
        pltpu.VMEM((levels, 1, lon), f32),
        pltpu.VMEM((levels, 1, lon), f32),
        pltpu.VMEM((levels, 1, lon), f32),
        pltpu.VMEM((levels, 1, lon), f32),
        pltpu.VMEM((1, lon), i32),
        pltpu.VMEM((1, lon), i32),
        pltpu.VMEM((levels, 7, 8, wide), f32),
        pltpu.VMEM((n_mem, chunks, 8, unit_wide), f32),
        pltpu.VMEM((count, unit_wide), f32),
        pltpu.VMEM((unit_wide, slots), jnp.bfloat16),
        pltpu.VMEM((n_mem, count // 2 // n_mem + 1, count), f32),
        pltpu.VMEM((n_mem - 1, count // 2 // n_mem + 1, count), f32),
        pltpu.VMEM((count // 2 // n_mem + 1, count), f32),
        pltpu.VMEM((y_ring - 1, count // 2 // n_mem + 1, count), f32),
        pltpu.VMEM((count // 2 // n_mem + 1, count), f32),
        pltpu.VMEM((z_ring - 1, count // 2 // n_mem + 1, count), f32),
        pltpu.VMEM((count // 2 // n_mem + 1, count), f32),
        pltpu.VMEM((n_mem, count // 2 // n_mem + 1, count), f32),
        pltpu.VMEM((n_mem, own, unit_wide), f32),
        pltpu.VMEM((levels, own, wide), f32),
    ]
    semaphores = [
        dma((9,)),
        dma((2, STEPS, chunks)), dma((2, STEPS, chunks)),
        dma((2, 3)), dma((2, 3)),
        dma((n_mem - 1, chunks)), dma((n_mem - 1, chunks)),
        dma((n_mem - 1,)), dma((n_mem - 1,)),
        dma((z_ring - 1,)), dma((z_ring - 1,)),
        dma((y_ring - 1,)), dma((y_ring - 1,)),
        dma((n_mem - 1,)), dma((n_mem - 1,)),
        dma((n_mem - 1,)), dma((n_mem - 1,)),
    ]
    result = pl.pallas_call(
        functools.partial(kernel, (n_grid, n_mem, z_ring, levels, lon, wide, chunks)),
        out_shape=pltpu.VMEM((levels, own, lon), f32),
        in_specs=[pl.BlockSpec(memory_space=pltpu.HBM)] * 9,
        out_specs=pl.BlockSpec(memory_space=pltpu.VMEM),
        scratch_shapes=scratch + semaphores,
        compiler_params=pltpu.CompilerParams(
            collective_id=0, has_side_effects=True, vmem_limit_bytes=60 * 1024 * 1024
        ),
    )(
        background_elapsed_years, currents, diffusivity, sea_mask, observed_cell, measured_layer_number, live_counts,
        observed_value, error_variance,
    )
    return result.transpose(1, 0, 2)[:, :, None, :]


def solution(mesh):
    placed = (
        P("mem", None, "grid", None),
        P(None, None, "grid", None),
        P(None, "grid", None),
        P("grid", None),
        P("grid"),
        P("grid"),
        P("grid"),
        P("grid"),
        P("grid"),
    )
    return jax.shard_map(
        functools.partial(per_device, mesh.shape["grid"], mesh.shape["mem"], Z_RING),
        mesh=mesh,
        in_specs=placed,
        out_specs=P("mem", None, "grid", None),
        check_vma=False,
    )
```
